32 devices in a mesh: batch: 4 (over x, core), space: 8 (over z, y).
Axes of the slice: x: 2, y: 2, z: 4, core: 2. Of those that a mesh axis runs over, the one named last changes fastest.
Arguments:
- inputs: bfloat16 [4, 32, 128, 128, 128], P('batch', None, None, 'space'), may hold values from -6 to 6
- pre_act: bfloat16 [4, 32, 128, 128, 128], P('batch', None, None, 'space'), may hold values from -8 to 8
- cotangent: bfloat16 [4, 32, 128, 128, 128], P('batch', None, None, 'space'), may hold values from -6 to 6
- spectral_weight: bfloat16 [2, 32, 32, 16384], P(None, None, None, 'space'), may hold values from -6 to 6
- skip_weight: bfloat16 [32, 32], replicated, may hold values from -1 to 1
Outputs:
- grad_inputs: bfloat16 [4, 32, 128, 128, 128], P('batch', None, None, 'space')
- grad_spectral: float32 [2, 32, 32, 16384], P(None, None, 'batch', 'space')
- grad_skip: float32 [32, 32], replicated
The draws below stay inside these ranges and needn't reach their ends.
All inputs are finite; a program needn't handle non-finite values.
Results may differ from the reference program's by a relative error of at most 0.0055.
Values sent between devices are 32-bit elements; how exact they have to be, the bound alone decides.
No kernel may reach another device: no remote copies, remote signals or barrier semaphores. Data moves between devices by JAX's collectives and lax.ppermute only.
A program may use at most 256 MiB of HBM per device.

```python
import math
import jax
import jax.numpy as jnp
from jax import lax

NX = 128
NY = 128
NZ = 128
CHANNELS = 32
MX = 16
MY = 16
MZ = 16
BATCH = 4
MODES = 16384


def shard_levels(own_key, shape, shards, least, largest):
    def one(position, shards_of):
        steps = jax.random.uniform(jax.random.fold_in(jax.random.fold_in(own_key, 6), position), (shards_of,), jnp.float32, least / len(shards), largest / len(shards))
        return jnp.repeat(jnp.exp(steps), shape[position] // shards_of).reshape((-1,) + (1,) * (len(shape) - position - 1))

    gain = one(*shards[0])
    for cut in shards[1:]:
        gain = gain * one(*cut)
    return gain


def centred(stream_key, shape, deviation, most, pieces=(), kind=jnp.bfloat16):
    loudness = shard_levels(stream_key, shape, pieces, -0.22, 0.18) if pieces else 1.0
    entries = jax.random.normal(stream_key, shape, jnp.float32) * deviation * loudness
    return jnp.minimum(jnp.maximum(entries, -most), most).astype(kind)


def setup_inputs(seed: int = 0) -> dict:
    streams_of = jax.random.split(jax.random.key(seed), 6)
    return {
        "inputs": centred(streams_of[0], (BATCH, CHANNELS, NX, NY, NZ), 1.0, 6.0, ((0, 4), (3, 8))),
        "pre_act": centred(streams_of[1], (BATCH, CHANNELS, NX, NY, NZ), 1.5, 8.0, ((0, 4), (3, 8))),
        "cotangent": centred(streams_of[2], (BATCH, CHANNELS, NX, NY, NZ), 1.0, 6.0, ((0, 4), (3, 8))),
        "spectral_weight": centred(streams_of[3], (2, CHANNELS, CHANNELS, MODES), 1.0, 6.0, ((3, 8),)),
        "skip_weight": centred(streams_of[4], (CHANNELS, CHANNELS), CHANNELS ** -0.5, 1.0),
    }


HIGHEST = lax.Precision.HIGHEST

def phase_table(length, count, signed):
    points = jnp.arange(length, dtype=jnp.int32)
    orders = jnp.arange(count, dtype=jnp.int32)
    if signed:
        orders = jnp.where(orders < count // 2, orders, orders - count)
    residues = jnp.mod(points[:, None] * orders[None, :], length)
    radians = residues.astype(jnp.float32) * (2.0 * math.pi / length)
    return (jnp.cos(radians), jnp.sin(radians))

def forward_block(cosine, sine):
    return jnp.stack([jnp.stack([cosine, -sine], axis=1), jnp.stack([sine, cosine], axis=1)], axis=0)

def inverse_block(cosine, sine):
    cos_rows = cosine.T
    sin_rows = sine.T
    return jnp.stack([jnp.stack([cos_rows, sin_rows], axis=1), jnp.stack([-sin_rows, cos_rows], axis=1)], axis=0)

def gelu_slope(values):
    normal_cdf = 0.5 * (1.0 + jax.scipy.special.erf(values * (1.0 / math.sqrt(2.0))))
    density = jnp.exp(-0.5 * values * values) * (1.0 / math.sqrt(2.0 * math.pi))
    return normal_cdf + values * density

def to_float(values):
    return lax.optimization_barrier(values.astype(jnp.bfloat16)).astype(jnp.float32)

def spectrum(grid_in):
    cos_x, sin_x = phase_table(NX, 2 * MX, True)
    table_x = to_float(jnp.stack([cos_x, -sin_x], axis=1))
    section_x = jnp.einsum('cxyz,xpa->cpayz', grid_in.astype(jnp.float32), table_x, precision=HIGHEST)
    cos_z, sin_z = phase_table(NZ, MZ, False)
    section_z = jnp.einsum('cpayz,pzqk->cqyak', section_x, forward_block(cos_z, sin_z), precision=HIGHEST)
    section_z = section_z.reshape(CHANNELS, 2, NY, 2 * MX * MZ)
    cos_y, sin_y = phase_table(NY, 2 * MY, True)
    section_y = jnp.einsum('cpym,pyqk->cqmk', section_z, forward_block(cos_y, sin_y), precision=HIGHEST)
    return section_y.reshape(CHANNELS, 2, MODES)

def back_transform(spectra):
    cos_y, sin_y = phase_table(NY, 2 * MY, True)
    shaped = spectra.reshape(CHANNELS, 2, 2 * MX * MZ, 2 * MY)
    grid_y = jnp.einsum('cpmk,pkqy->cqym', shaped, inverse_block(cos_y, sin_y), precision=HIGHEST)
    grid_y = grid_y.reshape(CHANNELS, 2, NY, 2 * MX, MZ)
    cos_z, sin_z = phase_table(NZ, MZ, False)
    grid_z = jnp.einsum('cpyak,pkqz->cqayz', grid_y, inverse_block(cos_z, sin_z), precision=HIGHEST)
    cos_x, sin_x = phase_table(NX, 2 * MX, True)
    table_x = jnp.stack([cos_x.T, -sin_x.T], axis=0)
    return jnp.einsum('cpayz,pax->cxyz', grid_z, table_x, precision=HIGHEST)

def mode_scale():
    kz_index = jnp.arange(MODES, dtype=jnp.int32) // (2 * MY) % MZ
    return jnp.where(kz_index == 0, 1.0, 2.0).astype(jnp.float32) / float(NX * NY * NZ)

def cross_terms(spec_left, spec_right):
    real_part = jnp.einsum('im,om->iom', spec_left[:, 0], spec_right[:, 0], precision=HIGHEST)
    real_part = real_part + jnp.einsum('im,om->iom', spec_left[:, 1], spec_right[:, 1], precision=HIGHEST)
    imag_part = jnp.einsum('im,om->iom', spec_left[:, 0], spec_right[:, 1], precision=HIGHEST)
    imag_part = imag_part - jnp.einsum('im,om->iom', spec_left[:, 1], spec_right[:, 0], precision=HIGHEST)
    return jnp.stack([real_part, imag_part], axis=0)

def reference(inputs, pre_act, cotangent, spectral_weight, skip_weight):
    weights_full = spectral_weight.astype(jnp.float32)
    skip_full = skip_weight.astype(jnp.float32)
    scales = mode_scale()

    def one_sample(running, sample):
        grad_modes, grad_mix = running
        grid_in, pre_grid, cot_grid = sample
        cot_pre = (cot_grid.astype(jnp.float32) * gelu_slope(pre_grid.astype(jnp.float32))).astype(jnp.bfloat16)
        spec_u = spectrum(grid_in)
        spec_e = spectrum(cot_pre)
        grad_modes = grad_modes + cross_terms(spec_u, spec_e)
        rounded = to_float(spec_e)
        back_real = jnp.einsum('iom,om->im', weights_full[0], rounded[:, 0], precision=HIGHEST)
        back_real = back_real + jnp.einsum('iom,om->im', weights_full[1], rounded[:, 1], precision=HIGHEST)
        back_imag = jnp.einsum('iom,om->im', weights_full[0], rounded[:, 1], precision=HIGHEST)
        back_imag = back_imag - jnp.einsum('iom,om->im', weights_full[1], rounded[:, 0], precision=HIGHEST)
        back_modes = jnp.stack([back_real, back_imag], axis=1) * scales
        spatial = back_transform(back_modes)
        cot_full = cot_pre.astype(jnp.float32)
        mixed = jnp.einsum('io,oxyz->ixyz', skip_full, cot_full, precision=HIGHEST)
        grad_grid = (spatial + mixed).astype(jnp.bfloat16)
        grad_mix = grad_mix + jnp.einsum('ixyz,oxyz->io', grid_in.astype(jnp.float32), cot_full, precision=HIGHEST)
        return ((grad_modes, grad_mix), grad_grid)
    start_state = (jnp.zeros((2, CHANNELS, CHANNELS, MODES), jnp.float32), jnp.zeros((CHANNELS, CHANNELS), jnp.float32))
    (grad_modes, grad_mix), grad_inputs = lax.scan(one_sample, start_state, (inputs, pre_act, cotangent))
    grad_spectral = grad_modes * scales
    grad_skip = grad_mix / math.sqrt(BATCH * NX * NY * NZ)
    return (grad_inputs, grad_spectral, grad_skip)
```

```python
import functools
import math

import jax
import jax.numpy as jnp
import ml_dtypes
import numpy as np
from jax import lax
from jax.experimental import pallas as pl
from jax.experimental.pallas import tpu as pltpu
from jax.sharding import PartitionSpec as P

NX = 128
NY = 128
NZ = 128
MX = 16
MY = 16
MZ = 16
GROUP = 8
LANES = GROUP * MZ
BF16 = jnp.bfloat16
F32 = jnp.float32
VMEM_LIMIT = 56 * 1024 * 1024


def waves(length, count, signed):
    points = np.arange(length)
    orders = np.arange(count)
    if signed:
        orders = np.where(orders < count // 2, orders, orders - count)
    radians = np.mod(points[:, None] * orders[None, :], length) * (2.0 * math.pi / length)
    return np.cos(radians), np.sin(radians)


def rounded_table(table):
    return np.asarray(table, np.float32).astype(ml_dtypes.bfloat16)


def z_forward_table():
    cos, sin = waves(NZ, MZ, False)
    table = np.zeros((GROUP, NZ, 2, GROUP, MZ))
    for c in range(GROUP):
        table[c, :, 0, c, :] = cos
        table[c, :, 1, c, :] = -sin
    return jnp.asarray(rounded_table(table.reshape(GROUP * NZ, 2 * LANES)))


def z_inverse_table():
    cos, sin = waves(NZ, MZ, False)
    table = np.zeros((2, GROUP, MZ, GROUP, NZ))
    for c in range(GROUP):
        table[0, c, :, c, :] = cos.T
        table[1, c, :, c, :] = -sin.T
    return jnp.asarray(rounded_table(table.reshape(2 * LANES, GROUP * NZ)))


def x_forward_table(spaces):
    cos, sin = waves(NX, 2 * MX, True)
    cos = cos.T.reshape(spaces, 2 * MX // spaces, NX)
    sin = sin.T.reshape(spaces, 2 * MX // spaces, NX)
    table = np.stack([np.stack([cos, sin], axis=2), np.stack([-sin, cos], axis=2)], axis=1)
    return jnp.asarray(rounded_table(table.reshape(4 * MX, 2 * NX)))


def x_inverse_table(spaces):
    cos, sin = waves(NX, 2 * MX, True)
    cos = cos.reshape(NX, spaces, 2 * MX // spaces)
    sin = sin.reshape(NX, spaces, 2 * MX // spaces)
    table = np.stack([np.stack([cos, -sin], axis=2), np.stack([sin, cos], axis=2)], axis=0)
    return jnp.asarray(rounded_table(table.reshape(2 * NX, 4 * MX)))


def split_pair(table):
    high = rounded_table(table)
    low = rounded_table(table - high.astype(np.float64))
    return jnp.asarray(high), jnp.asarray(low)


def y_forward_table(kx_local):
    cos, sin = waves(NY, 2 * MY, True)
    table = np.zeros((2, kx_local, 2 * MY, NY, 2, kx_local))
    for j in range(kx_local):
        table[0, j, :, :, 0, j] = cos.T
        table[0, j, :, :, 1, j] = sin.T
        table[1, j, :, :, 0, j] = -sin.T
        table[1, j, :, :, 1, j] = cos.T
    return split_pair(table.reshape(4 * MY * kx_local, 2 * NY * kx_local))


def y_inverse_table(kx_local):
    cos, sin = waves(NY, 2 * MY, True)
    table = np.zeros((NY, 2, kx_local, 2, kx_local, 2 * MY))
    for j in range(kx_local):
        table[:, 0, j, 0, j, :] = cos
        table[:, 0, j, 1, j, :] = -sin
        table[:, 1, j, 0, j, :] = sin
        table[:, 1, j, 1, j, :] = cos
    return split_pair(table.reshape(2 * NY * kx_local, 4 * MY * kx_local))


def dot(left, right):
    return lax.dot_general(left, right, (((1,), (0,)), ((), ())), preferred_element_type=F32)


def dot_split(table_high, table_low, values):
    high = values.astype(BF16)
    low = (values - high.astype(F32)).astype(BF16)
    return dot(table_high, high) + dot(table_high, low) + dot(table_low, high)


def params(count=1):
    return pltpu.CompilerParams(
        vmem_limit_bytes=VMEM_LIMIT, dimension_semantics=("arbitrary",) * count
    )


def z_then_x(load, table_z, table_x, send_ref, real_ref, imag_ref, planes, spaces):
    rows = NX * planes
    step = min(rows, 512)
    for start in range(0, rows, step):
        line = jnp.concatenate([load(c, start, step) for c in range(GROUP)], axis=1)
        found = dot(line, table_z[...])
        real_ref[start : start + step, :] = found[:, :LANES]
        imag_ref[start : start + step, :] = found[:, LANES:]
    part = 4 * MX // spaces
    for y in range(0, planes, 2):
        pair = []
        for at in (y, y + 1):
            real = real_ref[pl.ds(at, NX, stride=planes), :]
            imag = imag_ref[pl.ds(at, NX, stride=planes), :]
            pair.append(jnp.concatenate([real, imag], axis=0).astype(BF16))
        found = dot(table_x[...], jnp.concatenate(pair, axis=1))
        for place in range(2):
            for s in range(spaces):
                send_ref[s, 0, (y + place) * part : (y + place + 1) * part, :] = found[
                    s * part : (s + 1) * part, place * LANES : (place + 1) * LANES
                ]


def forward_plain(field_ref, table_z, table_x, send_ref, real_ref, imag_ref, *, planes, spaces):
    def load(c, start, step):
        return field_ref[c, start : start + step, :]

    z_then_x(load, table_z, table_x, send_ref, real_ref, imag_ref, planes, spaces)


def slope(values):
    normal_cdf = 0.5 * (1.0 + lax.erf(values * (1.0 / math.sqrt(2.0))))
    density = jnp.exp(-0.5 * values * values) * (1.0 / math.sqrt(2.0 * math.pi))
    return normal_cdf + values * density


def forward_cot(
    pre_ref, cot_ref, table_z, table_x, send_ref, out_ref, real_ref, imag_ref, *, planes, spaces
):
    def load(c, start, step):
        pre = pre_ref[c, start : start + step, :].astype(F32)
        cot = cot_ref[c, start : start + step, :].astype(F32)
        made = (cot * slope(pre)).astype(BF16)
        out_ref[c, start : start + step, :] = made
        return made

    z_then_x(load, table_z, table_x, send_ref, real_ref, imag_ref, planes, spaces)


def whole(shape):
    return pl.BlockSpec(shape, lambda *_: (0,) * len(shape))


def forward(fields, planes, spaces, cot):
    channels, rows, _ = fields[0].shape
    groups = channels // GROUP
    part = 4 * MX // spaces
    field_spec = pl.BlockSpec((GROUP, rows, NZ), lambda g: (g, 0, 0))
    send_shape = jax.ShapeDtypeStruct((spaces, groups, planes * part, LANES), F32)
    send_spec = pl.BlockSpec((spaces, 1, planes * part, LANES), lambda g: (0, g, 0, 0))
    out_shape, out_specs = (send_shape,), (send_spec,)
    if cot:
        out_shape += (jax.ShapeDtypeStruct(fields[0].shape, BF16),)
        out_specs += (field_spec,)
    return pl.pallas_call(
        functools.partial(forward_cot if cot else forward_plain, planes=planes, spaces=spaces),
        out_shape=out_shape,
        grid=(groups,),
        in_specs=[field_spec] * len(fields)
        + [whole((GROUP * NZ, 2 * LANES)), whole((4 * MX, 2 * NX))],
        out_specs=out_specs,
        scratch_shapes=[pltpu.VMEM((rows, LANES), F32), pltpu.VMEM((rows, LANES), F32)],
        compiler_params=params(),
        cost_estimate=pl.CostEstimate(
            flops=2 * 8 * channels * rows * NZ * 4 * MZ,
            bytes_accessed=2 * len(fields) * channels * rows * NZ,
            transcendentals=0,
        ),
        name="forward_e" if cot else "forward_u",
    )(*fields, z_forward_table(), x_forward_table(spaces))


def unfold_y(received_ref, high, low, lines, store, groups, kx_local):
    width = kx_local * 2 * MY
    for g in range(groups):
        data = received_ref[:, g].reshape(-1, LANES)
        found = dot_split(high[...], low[...], data)
        for part in range(2):
            lines[part, g * LANES : (g + 1) * LANES, :] = found[
                part * width : (part + 1) * width, :
            ].T
    channels = groups * GROUP
    for part in range(2):
        for kz in range(MZ):
            piece = lines[part, pl.ds(kz, channels, stride=MZ), :]
            for j in range(kx_local):
                store(
                    part,
                    (j * MZ + kz) * 2 * MY,
                    piece[:, j * 2 * MY : (j + 1) * 2 * MY],
                )


def spectrum_u(received_ref, high, low, hat_ref, lines, *, groups, kx_local):
    def store(part, column, values):
        hat_ref[part, :, column : column + 2 * MY] = values

    unfold_y(received_ref, high, low, lines, store, groups, kx_local)


def finish_u(received, kx_local):
    spaces, groups, rows, _ = received.shape
    channels = groups * GROUP
    modes = kx_local * MZ * 2 * MY
    high, low = y_forward_table(kx_local)
    return pl.pallas_call(
        functools.partial(spectrum_u, groups=groups, kx_local=kx_local),
        out_shape=jax.ShapeDtypeStruct((2, channels, modes), F32),
        scratch_shapes=[pltpu.VMEM((2, channels * MZ, kx_local * 2 * MY), F32)],
        compiler_params=pltpu.CompilerParams(vmem_limit_bytes=VMEM_LIMIT),
        name="finish_u",
    )(received, high, low)


def spectrum_e(
    received_ref,
    weight_ref,
    high,
    low,
    inv_high,
    inv_low,
    hat_ref,
    send_ref,
    lines,
    rounded,
    back,
    *,
    groups,
    kx_local,
    per_step,
):
    step = pl.program_id(0)
    channels = groups * GROUP
    modes = kx_local * MZ * 2 * MY
    width = kx_local * 2 * MY

    @pl.when(step == 0)
    def _():
        def store(part, column, values):
            hat_ref[part, :, column : column + 2 * MY] = values
            kz = (column // (2 * MY)) % MZ
            scale = (1.0 if kz == 0 else 2.0) / float(NX * NY * NZ)
            rounded[part, :, column : column + 2 * MY] = values.astype(BF16).astype(F32) * scale

        unfold_y(received_ref, high, low, lines, store, groups, kx_local)

    tile = min(modes, 512)
    for i in range(per_step):
        for start in range(0, modes, tile):
            lane = slice(start, start + tile)
            real = rounded[0, :, lane]
            imag = rounded[1, :, lane]
            weight_real = weight_ref[0, i, :, lane].astype(F32)
            weight_imag = weight_ref[1, i, :, lane].astype(F32)
            row = step * per_step + i
            back[0, pl.ds(row, 1), lane] = jnp.sum(
                weight_real * real + weight_imag * imag, axis=0, keepdims=True
            )
            back[1, pl.ds(row, 1), lane] = jnp.sum(
                weight_real * imag - weight_imag * real, axis=0, keepdims=True
            )

    @pl.when(step == pl.num_programs(0) - 1)
    def _():
        for part in range(2):
            for kz in range(MZ):
                pieces = [
                    back[part, :, (j * MZ + kz) * 2 * MY : (j * MZ + kz + 1) * 2 * MY]
                    for j in range(kx_local)
                ]
                lines[part, pl.ds(kz, channels, stride=MZ), :] = jnp.concatenate(pieces, axis=1)
        for g in range(groups):
            data = jnp.concatenate(
                [lines[part, g * LANES : (g + 1) * LANES, :].T for part in range(2)], axis=0
            )
            found = dot_split(inv_high[...], inv_low[...], data)
            send_ref[:, g] = found.reshape(send_ref.shape[0], -1, LANES)


def finish_e(received, weight, kx_local):
    spaces, groups, rows, _ = received.shape
    channels = groups * GROUP
    modes = kx_local * MZ * 2 * MY
    per_step = 4
    high, low = y_forward_table(kx_local)
    inv_high, inv_low = y_inverse_table(kx_local)
    return pl.pallas_call(
        functools.partial(spectrum_e, groups=groups, kx_local=kx_local, per_step=per_step),
        out_shape=(
            jax.ShapeDtypeStruct((2, channels, modes), F32),
            jax.ShapeDtypeStruct(received.shape, F32),
        ),
        grid=(channels // per_step,),
        in_specs=[
            whole(received.shape),
            pl.BlockSpec((2, per_step, channels, modes), lambda i: (0, i, 0, 0)),
            whole(high.shape),
            whole(low.shape),
            whole(inv_high.shape),
            whole(inv_low.shape),
        ],
        out_specs=(whole((2, channels, modes)), whole(received.shape)),
        scratch_shapes=[
            pltpu.VMEM((2, channels * MZ, kx_local * 2 * MY), F32),
            pltpu.VMEM((2, channels, modes), F32),
            pltpu.VMEM((2, channels, modes), F32),
        ],
        compiler_params=params(),
        name="finish_e",
    )(received, weight, high, low, inv_high, inv_low)


def mix_body(input_ref, cot_ref, spread_ref, mixed_ref, skip_ref, total, *, planes, count):
    step = pl.program_id(0)
    channels = input_ref.shape[0]
    side = channels * planes

    @pl.when(step == 0)
    def _():
        total[...] = jnp.zeros_like(total)

    cots, lefts = [], []
    for k in range(count):
        rows = slice(k * planes, (k + 1) * planes)
        cots.append(cot_ref[:, rows, :].reshape(side, NZ))
        lefts.append(input_ref[:, rows, :].reshape(side, NZ))
    cot = jnp.concatenate(cots, axis=1)
    left = jnp.concatenate(lefts, axis=1)
    total[...] += lax.dot_general(
        left, cot, (((1,), (1,)), ((), ())), preferred_element_type=F32
    )
    mixed = dot(spread_ref[...], cot).astype(BF16)
    for k in range(count):
        mixed_ref[:, k * planes : (k + 1) * planes, :] = mixed[
            :, k * NZ : (k + 1) * NZ
        ].reshape(channels, planes, NZ)

    @pl.when(step == pl.num_programs(0) - 1)
    def _():
        row = lax.broadcasted_iota(jnp.int32, (side, side), 0)
        column = lax.broadcasted_iota(jnp.int32, (side, side), 1)
        kept = jnp.where(row % planes == column % planes, total[...], 0.0)
        pick = (
            lax.broadcasted_iota(jnp.int32, (side, channels), 0) // planes
            == lax.broadcasted_iota(jnp.int32, (side, channels), 1)
        ).astype(F32)
        half = lax.dot_general(
            kept, pick, (((1,), (0,)), ((), ())), precision=lax.Precision.HIGHEST,
            preferred_element_type=F32,
        )
        skip_ref[...] = lax.dot_general(
            pick, half, (((0,), (0,)), ((), ())), precision=lax.Precision.HIGHEST,
            preferred_element_type=F32,
        )


def mix(inputs, cot, spread, planes):
    channels, rows, _ = inputs.shape
    count = 4
    side = channels * planes
    spec = pl.BlockSpec((channels, count * planes, NZ), lambda x: (0, x, 0))
    return pl.pallas_call(
        functools.partial(mix_body, planes=planes, count=count),
        out_shape=(
            jax.ShapeDtypeStruct(inputs.shape, BF16),
            jax.ShapeDtypeStruct((channels, channels), F32),
        ),
        grid=(NX // count,),
        in_specs=[spec, spec, whole((side, side))],
        out_specs=(spec, whole((channels, channels))),
        scratch_shapes=[pltpu.VMEM((side, side), F32)],
        compiler_params=params(),
        cost_estimate=pl.CostEstimate(
            flops=4 * NX * side * side * NZ,
            bytes_accessed=6 * channels * rows * NZ,
            transcendentals=0,
        ),
        name="mix",
    )(inputs, cot, spread)


def to_grid_body(
    received_ref, mixed_ref, table_x, table_z, out_ref, real_ref, imag_ref, *, planes, spaces
):
    part = 4 * MX // spaces
    rows = NX * planes
    for y in range(0, planes, 2):
        pair = [
            jnp.concatenate(
                [received_ref[s, 0, at * part : (at + 1) * part, :] for s in range(spaces)], axis=0
            ).astype(BF16)
            for at in (y, y + 1)
        ]
        found = dot(table_x[...], jnp.concatenate(pair, axis=1))
        for place in range(2):
            lane = slice(place * LANES, (place + 1) * LANES)
            real_ref[pl.ds(y + place, NX, stride=planes), :] = found[:NX, lane]
            imag_ref[pl.ds(y + place, NX, stride=planes), :] = found[NX:, lane]
    step = min(rows, 256)
    for start in range(0, rows, step):
        line = jnp.concatenate(
            [real_ref[start : start + step, :], imag_ref[start : start + step, :]], axis=1
        ).astype(BF16)
        found = dot(line, table_z[...])
        for c in range(GROUP):
            mixed = mixed_ref[c, start : start + step, :].astype(F32)
            out_ref[c, start : start + step, :] = (
                found[:, c * NZ : (c + 1) * NZ] + mixed
            ).astype(BF16)


def grid_of(received, mixed, planes):
    spaces, groups, rows, _ = received.shape
    spec = pl.BlockSpec((GROUP, NX * planes, NZ), lambda g: (g, 0, 0))
    return pl.pallas_call(
        functools.partial(to_grid_body, planes=planes, spaces=spaces),
        out_shape=jax.ShapeDtypeStruct(mixed.shape, BF16),
        grid=(groups,),
        in_specs=[
            pl.BlockSpec((spaces, 1, rows, LANES), lambda g: (0, g, 0, 0)),
            spec,
            whole((2 * NX, 4 * MX)),
            whole((2 * LANES, GROUP * NZ)),
        ],
        out_specs=spec,
        scratch_shapes=[
            pltpu.VMEM((NX * planes, LANES), F32),
            pltpu.VMEM((NX * planes, LANES), F32),
        ],
        input_output_aliases={1: 0},
        compiler_params=params(),
        name="to_grid",
    )(received, mixed, x_inverse_table(spaces), z_inverse_table())


def cross_body(left_ref, right_ref, out_ref, *, samples):
    lanes = out_ref.shape[-1]
    channels = left_ref.shape[2]
    own = right_ref.shape[2]
    kz = lax.broadcasted_iota(jnp.int32, (own, lanes), 1) // (2 * MY) % MZ
    scale = jnp.where(kz == 0, 1.0, 2.0) / float(NX * NY * NZ)
    rights = [
        (right_ref[b, 0] * scale, right_ref[b, 1] * scale) for b in range(samples)
    ]
    for i in range(channels):
        real = imag = None
        for b in range(samples):
            left_real = left_ref[b, 0, i : i + 1, :]
            left_imag = left_ref[b, 1, i : i + 1, :]
            right_real, right_imag = rights[b]
            one = left_real * right_real + left_imag * right_imag
            two = left_real * right_imag - left_imag * right_real
            real = one if real is None else real + one
            imag = two if imag is None else imag + two
        out_ref[0, i] = real
        out_ref[1, i] = imag


def cross(left, right):
    samples, _, channels, modes = left.shape
    own = right.shape[2]
    lanes = 2 * MY * MZ
    return pl.pallas_call(
        functools.partial(cross_body, samples=samples),
        out_shape=jax.ShapeDtypeStruct((2, channels, own, modes), F32),
        grid=(modes // lanes,),
        in_specs=[
            pl.BlockSpec((samples, 2, channels, lanes), lambda k: (0, 0, 0, k)),
            pl.BlockSpec((samples, 2, own, lanes), lambda k: (0, 0, 0, k)),
        ],
        out_specs=pl.BlockSpec((2, channels, own, lanes), lambda k: (0, 0, 0, k)),
        compiler_params=params(),
        name="cross",
    )(left, right)


def exchange(values):
    return lax.all_to_all(values, "space", split_axis=0, concat_axis=0, tiled=True)


HIGHEST = lax.Precision.HIGHEST


def phase_table(length, count, signed):
    points = jnp.arange(length, dtype=jnp.int32)
    orders = jnp.arange(count, dtype=jnp.int32)
    if signed:
        orders = jnp.where(orders < count // 2, orders, orders - count)
    residues = jnp.mod(points[:, None] * orders[None, :], length)
    radians = residues.astype(jnp.float32) * (2.0 * math.pi / length)
    return (jnp.cos(radians), jnp.sin(radians))


def forward_block(cosine, sine):
    return jnp.stack(
        [jnp.stack([cosine, -sine], axis=1), jnp.stack([sine, cosine], axis=1)], axis=0
    )


def inverse_block(cosine, sine):
    cos_rows = cosine.T
    sin_rows = sine.T
    return jnp.stack(
        [jnp.stack([cos_rows, sin_rows], axis=1), jnp.stack([-sin_rows, cos_rows], axis=1)], axis=0
    )


def local_spectrum(grid_in):
    cos_x, sin_x = phase_table(NX, 2 * MX, True)
    table_x = jnp.stack([cos_x, -sin_x], axis=1).astype(jnp.bfloat16)
    section_x = jnp.einsum(
        "scxyz,xpa->scpayz", grid_in, table_x, preferred_element_type=jnp.float32
    )
    cos_z, sin_z = phase_table(NZ, MZ, False)
    section_z = jnp.einsum(
        "scpayz,pzqk->scqyak", section_x, forward_block(cos_z, sin_z), precision=HIGHEST
    )
    return section_z.reshape(
        section_z.shape[0], section_z.shape[1], 2, section_z.shape[3], 2 * MX * MZ
    )


def along_y(spectra):
    cos_y, sin_y = phase_table(NY, 2 * MY, True)
    section_y = jnp.einsum(
        "scpym,pyqk->scqmk", spectra, forward_block(cos_y, sin_y), precision=HIGHEST
    )
    return section_y.reshape(section_y.shape[0], section_y.shape[1], 2, section_y.shape[3] * 2 * MY)


def both_along_y(spectra_pair):
    return (along_y(spectra_pair[0]), along_y(spectra_pair[1]))


def to_grid(spectra):
    shaped = spectra.reshape(spectra.shape[0], spectra.shape[1], 2, spectra.shape[3], 2 * MX, MZ)
    cos_z, sin_z = phase_table(NZ, MZ, False)
    grid_z = jnp.einsum(
        "scpyak,pkqz->scqayz", shaped, inverse_block(cos_z, sin_z), precision=HIGHEST
    )
    cos_x, sin_x = phase_table(NX, 2 * MX, True)
    table_x = jnp.stack([cos_x.T, -sin_x.T], axis=0)
    return jnp.einsum("scpayz,pax->scxyz", grid_z, table_x, precision=HIGHEST)


def cross_terms(spec_left, spec_right):
    real_part = jnp.einsum(
        "sim,som->iom", spec_left[:, :, 0], spec_right[:, :, 0], precision=HIGHEST
    )
    real_part = real_part + jnp.einsum(
        "sim,som->iom", spec_left[:, :, 1], spec_right[:, :, 1], precision=HIGHEST
    )
    imag_part = jnp.einsum(
        "sim,som->iom", spec_left[:, :, 0], spec_right[:, :, 1], precision=HIGHEST
    )
    imag_part = imag_part - jnp.einsum(
        "sim,som->iom", spec_left[:, :, 1], spec_right[:, :, 0], precision=HIGHEST
    )
    return jnp.stack([real_part, imag_part], axis=0)


def contract(weight_part, spec_part):
    return jnp.einsum("iom,som->sim", weight_part, spec_part, preferred_element_type=jnp.float32)


def skip_gradient(grid_in, cot_pre):
    partial_sum = jnp.einsum(
        "sixyz,soxyz->io", grid_in, cot_pre, preferred_element_type=jnp.float32
    )
    summed = lax.psum(partial_sum, ("batch", "space"))
    return summed / math.sqrt(grid_in.shape[0] * lax.axis_size("batch") * NX * NY * NZ)


def general(inputs, pre_act, cotangent, spectral_weight, skip_weight):
    samples = inputs.shape[0]
    channels = inputs.shape[1]
    slope_pre = slope(pre_act.astype(jnp.float32))
    cot_pre = (cotangent.astype(jnp.float32) * slope_pre).astype(jnp.bfloat16)
    spec_u, spec_e = both_along_y(
        (
            lax.all_to_all(
                local_spectrum(inputs), "space", split_axis=4, concat_axis=3, tiled=True
            ),
            lax.all_to_all(
                local_spectrum(cot_pre), "space", split_axis=4, concat_axis=3, tiled=True
            ),
        )
    )
    mode_count = spec_u.shape[3]
    position = jnp.arange(mode_count, dtype=jnp.int32)
    kxz_index = lax.axis_index("space") * (mode_count // (2 * MY)) + position // (2 * MY)
    mode_weights = jnp.where(kxz_index % MZ == 0, 1.0, 2.0).astype(jnp.float32) / float(
        NX * NY * NZ
    )
    mode_grad = lax.psum_scatter(
        cross_terms(spec_u, spec_e), "batch", scatter_dimension=2, tiled=True
    )
    grad_spectral = mode_grad * mode_weights
    rounded = spec_e.astype(jnp.bfloat16)
    weight_real = spectral_weight[0]
    weight_imag = spectral_weight[1]
    back_real = contract(weight_real, rounded[:, :, 0]) + contract(weight_imag, rounded[:, :, 1])
    back_imag = contract(weight_real, rounded[:, :, 1]) - contract(weight_imag, rounded[:, :, 0])
    back_modes = jnp.stack([back_real, back_imag], axis=2) * mode_weights
    shaped = back_modes.reshape(samples, channels, 2, mode_count // (2 * MY), 2 * MY)
    cos_y, sin_y = phase_table(NY, 2 * MY, True)
    grid_y = jnp.einsum("scpmk,pkqy->scqym", shaped, inverse_block(cos_y, sin_y), precision=HIGHEST)
    spatial = to_grid(lax.all_to_all(grid_y, "space", split_axis=3, concat_axis=4, tiled=True))
    mixed = jnp.einsum("io,soxyz->sixyz", skip_weight, cot_pre, preferred_element_type=jnp.float32)
    grad_inputs = (spatial + mixed).astype(jnp.bfloat16)
    grad_skip = skip_gradient(inputs, cot_pre)
    return (grad_inputs, grad_spectral, grad_skip)


def on_device(inputs, pre_act, cotangent, spectral_weight, skip_weight):
    samples, channels, _, planes, _ = inputs.shape
    spaces = lax.axis_size("space")
    batches = lax.axis_size("batch")
    if samples != 1 or (2 * MX) % spaces or planes % 16 or channels % GROUP:
        return general(inputs, pre_act, cotangent, spectral_weight, skip_weight)
    kx_local = 2 * MX // spaces
    flat = (channels, NX * planes, NZ)
    inputs, pre_act, cotangent = (v.reshape(flat) for v in (inputs, pre_act, cotangent))
    (send_u,) = forward((inputs,), planes, spaces, False)
    received_u = exchange(send_u)
    send_e, cot_pre = forward((pre_act, cotangent), planes, spaces, True)
    received_e = exchange(send_e)
    spread = jnp.einsum("io,yv->iyov", skip_weight, jnp.eye(planes, dtype=BF16))
    spread = spread.reshape(channels * planes, channels * planes)
    mixed, skip_part = mix(inputs, cot_pre, spread, planes)
    skip_all = lax.all_gather(skip_part, ("batch", "space"))
    hat_u = finish_u(received_u, kx_local)
    all_u = lax.all_gather(hat_u, "batch")
    hat_e, send_back = finish_e(received_e, spectral_weight, kx_local)
    own = channels // batches
    modes = hat_e.shape[-1]
    parts_e = hat_e.reshape(2, batches, own, modes).swapaxes(0, 1)
    own_e = lax.all_to_all(parts_e, "batch", split_axis=0, concat_axis=0, tiled=True)
    received_back = exchange(send_back)
    grad_spectral = cross(all_u, own_e)
    grad_inputs = grid_of(received_back, mixed, planes)
    grad_skip = jnp.sum(skip_all, axis=0) / math.sqrt(samples * batches * NX * NY * NZ)
    return (
        grad_inputs.reshape(samples, channels, NX, planes, NZ),
        grad_spectral,
        grad_skip,
    )


def solution(mesh):
    placed = (
        P("batch", None, None, "space", None),
        P("batch", None, None, "space", None),
        P("batch", None, None, "space", None),
        P(None, None, None, "space"),
        P(),
    )
    return jax.shard_map(
        on_device,
        mesh=mesh,
        in_specs=placed,
        out_specs=(P("batch", None, None, "space", None), P(None, None, "batch", "space"), P()),
        check_vma=False,
    )
```

```python
import functools
import math

import jax
import jax.numpy as jnp
import ml_dtypes
import numpy as np
from jax import lax
from jax.experimental import pallas as pl
from jax.experimental.pallas import tpu as pltpu
from jax.sharding import PartitionSpec as P

NX = 128
NY = 128
NZ = 128
MX = 16
MY = 16
MZ = 16
GROUP = 8
LANES = GROUP * MZ
BF16 = jnp.bfloat16
F32 = jnp.float32
VMEM_LIMIT = 56 * 1024 * 1024


def cost(microseconds):
    return pl.CostEstimate(flops=int(microseconds * 2e9), bytes_accessed=1, transcendentals=0)


def waves(length, count, signed):
    points = np.arange(length)
    orders = np.arange(count)
    if signed:
        orders = np.where(orders < count // 2, orders, orders - count)
    radians = np.mod(points[:, None] * orders[None, :], length) * (2.0 * math.pi / length)
    return np.cos(radians), np.sin(radians)


def rounded_table(table):
    return np.asarray(table, np.float32).astype(ml_dtypes.bfloat16)


def z_forward_table():
    cos, sin = waves(NZ, MZ, False)
    table = np.zeros((GROUP, NZ, 2, GROUP, MZ))
    for c in range(GROUP):
        table[c, :, 0, c, :] = cos
        table[c, :, 1, c, :] = -sin
    return jnp.asarray(rounded_table(table.reshape(GROUP * NZ, 2 * LANES)))


def z_inverse_table():
    cos, sin = waves(NZ, MZ, False)
    table = np.zeros((2, GROUP, MZ, GROUP, NZ))
    for c in range(GROUP):
        table[0, c, :, c, :] = cos.T
        table[1, c, :, c, :] = -sin.T
    return jnp.asarray(rounded_table(table.reshape(2 * LANES, GROUP * NZ)))


def x_forward_table(spaces):
    cos, sin = waves(NX, 2 * MX, True)
    cos = cos.T.reshape(spaces, 2 * MX // spaces, NX)
    sin = sin.T.reshape(spaces, 2 * MX // spaces, NX)
    table = np.stack([np.stack([cos, sin], axis=2), np.stack([-sin, cos], axis=2)], axis=1)
    return jnp.asarray(rounded_table(table.reshape(4 * MX, 2 * NX)))


def x_inverse_table(spaces):
    cos, sin = waves(NX, 2 * MX, True)
    cos = cos.reshape(NX, spaces, 2 * MX // spaces)
    sin = sin.reshape(NX, spaces, 2 * MX // spaces)
    table = np.stack([np.stack([cos, -sin], axis=2), np.stack([sin, cos], axis=2)], axis=0)
    return jnp.asarray(rounded_table(table.reshape(2 * NX, 4 * MX)))


def split_table(table):
    high = rounded_table(table)
    low = rounded_table(table - high.astype(np.float64))
    return jnp.asarray(np.concatenate([high, high, low], axis=-1))


def y_forward_table(kx_local):
    cos, sin = waves(NY, 2 * MY, True)
    table = np.zeros((2, kx_local, 2 * MY, NY, 2, kx_local))
    for j in range(kx_local):
        table[0, j, :, :, 0, j] = cos.T
        table[0, j, :, :, 1, j] = sin.T
        table[1, j, :, :, 0, j] = -sin.T
        table[1, j, :, :, 1, j] = cos.T
    table = table.reshape(4 * MY * kx_local, 2, NY * kx_local)
    return split_table(table.swapaxes(0, 1))


def y_inverse_table(kx_local):
    cos, sin = waves(NY, 2 * MY, True)
    table = np.zeros((NY, 2, kx_local, 2, kx_local, 2 * MY))
    for j in range(kx_local):
        table[:, 0, j, 0, j, :] = cos
        table[:, 0, j, 1, j, :] = -sin
        table[:, 1, j, 0, j, :] = sin
        table[:, 1, j, 1, j, :] = cos
    return split_table(table.reshape(2, NY * kx_local, 4 * MY * kx_local))


def dot(left, right):
    return lax.dot_general(left, right, (((1,), (0,)), ((), ())), preferred_element_type=F32)


def dot_split(table, values):
    high = values.astype(BF16)
    low = (values - high.astype(F32)).astype(BF16)
    return dot(table, jnp.concatenate([high, low, high], axis=0))


def params(count=1):
    return pltpu.CompilerParams(
        vmem_limit_bytes=VMEM_LIMIT, dimension_semantics=("arbitrary",) * count
    )


def z_then_x(load, table_z, table_x, send_ref, real_ref, imag_ref, planes, spaces, blocks):
    rows = NX * planes // blocks
    block = pl.program_id(1)
    step = min(rows, 512)
    for start in range(0, rows, step):
        line = jnp.concatenate([load(c, start, step) for c in range(GROUP)], axis=1)
        found = dot(line, table_z[...])
        place = pl.ds(pl.multiple_of(block * rows + start, step), step)
        real_ref[place, :] = found[:, :LANES]
        imag_ref[place, :] = found[:, LANES:]
    part = 4 * MX // spaces

    @pl.when(block == blocks - 1)
    def _():
        for y in range(0, planes, 2):
            pair = []
            for at in (y, y + 1):
                real = real_ref[pl.ds(at, NX, stride=planes), :]
                imag = imag_ref[pl.ds(at, NX, stride=planes), :]
                pair.append(jnp.concatenate([real, imag], axis=0).astype(BF16))
            found = dot(table_x[...], jnp.concatenate(pair, axis=1))
            for place in range(2):
                for s in range(spaces):
                    relay, side = s % (spaces // 2), s // (spaces // 2)
                    rows_of = slice((y + place) * part, (y + place + 1) * part)
                    send_ref[relay, side, rows_of, :] = found[
                        s * part : (s + 1) * part, place * LANES : (place + 1) * LANES
                    ]


def forward_plain(
    field_ref, table_z, table_x, *refs, planes, spaces, blocks
):
    send_ref, real_ref, imag_ref = refs[-3:]

    def load(c, start, step):
        return field_ref[c, start : start + step, :]

    z_then_x(load, table_z, table_x, send_ref, real_ref, imag_ref, planes, spaces, blocks)


def slope(values):
    normal_cdf = 0.5 * (1.0 + lax.erf(values * (1.0 / math.sqrt(2.0))))
    density = jnp.exp(-0.5 * values * values) * (1.0 / math.sqrt(2.0 * math.pi))
    return normal_cdf + values * density


def forward_cot(pre_ref, cot_ref, table_z, table_x, *refs, planes, spaces, blocks):
    send_ref, out_ref, real_ref, imag_ref = refs[-4:]

    def load(c, start, step):
        pre = pre_ref[c, start : start + step, :].astype(F32)
        cot = cot_ref[c, start : start + step, :].astype(F32)
        made = (cot * slope(pre)).astype(BF16)
        out_ref[c, start : start + step, :] = made
        return made

    z_then_x(load, table_z, table_x, send_ref, real_ref, imag_ref, planes, spaces, blocks)


def whole(shape):
    return pl.BlockSpec(shape, lambda *_: (0,) * len(shape))


ANYWHERE = pl.BlockSpec(memory_space=pl.ANY)


def forward(fields, first, groups, planes, spaces, cot, after=()):
    channels, rows, _ = fields[0].shape
    blocks = 1
    part = 4 * MX // spaces
    field_spec = pl.BlockSpec((GROUP, rows // blocks, NZ), lambda g, r: (g + first, r, 0))
    send_shape = jax.ShapeDtypeStruct((spaces // 2, 2, groups * planes * part, LANES), F32)
    send_spec = pl.BlockSpec((spaces // 2, 2, planes * part, LANES), lambda g, r: (0, 0, g, 0))
    out_shape, out_specs = (send_shape,), (send_spec,)
    if cot:
        out_shape += (jax.ShapeDtypeStruct(fields[0].shape, BF16),)
        out_specs += (field_spec,)
    body = forward_cot if cot else forward_plain
    return pl.pallas_call(
        functools.partial(body, planes=planes, spaces=spaces, blocks=blocks),
        out_shape=out_shape,
        grid=(groups, blocks),
        in_specs=[field_spec] * len(fields)
        + [whole((GROUP * NZ, 2 * LANES)), whole((4 * MX, 2 * NX))]
        + [ANYWHERE] * len(after),
        out_specs=out_specs,
        scratch_shapes=[pltpu.VMEM((rows, LANES), F32), pltpu.VMEM((rows, LANES), F32)],
        compiler_params=params(2),
        cost_estimate=cost(25 if cot else 11),
        name="forward_e" if cot else "forward_u",
    )(*fields, z_forward_table(), x_forward_table(spaces), *after)


def half_sums(near_ref, table, g, count):
    relays = near_ref.shape[0]
    per_group = table.shape[2] // 3 // relays
    data = jnp.concatenate(
        [
            jnp.concatenate(
                [
                    near_ref[r, 0, at * per_group : (at + 1) * per_group, :]
                    for at in range(g, g + count)
                ],
                axis=1,
            )
            for r in range(relays)
        ],
        axis=0,
    )
    return dot_split(table[0], data)


def partial_body(half_ref, near_ref, table, *refs):
    out_ref = refs[-1]
    for g in range(0, out_ref.shape[0], 2):
        found = half_sums(near_ref, table, g, 2)
        out_ref[g] = found[:, :LANES]
        out_ref[g + 1] = found[:, LANES:]


def table_spec(table, side):
    return pl.BlockSpec((1,) + table.shape[1:], lambda *at: (side(at[-1][0]), 0, 0))


def near_spec(near, side):
    shape = (near.shape[0], 1) + near.shape[2:]
    return pl.BlockSpec(shape, lambda *at: (0, side(at[-1][0]), 0, 0))


def own_side(half):
    return half


def other_side(half):
    return 1 - half


def fixed(shape):
    return pl.BlockSpec(shape, lambda *at: (0,) * len(shape))


def partial_sums(half, near, groups, kx_local, name, after=()):
    table = y_forward_table(kx_local)
    shape = (groups, table.shape[1], LANES)
    return pl.pallas_call(
        partial_body,
        out_shape=jax.ShapeDtypeStruct(shape, F32),
        grid_spec=pltpu.PrefetchScalarGridSpec(
            num_scalar_prefetch=1,
            grid=(1,),
            in_specs=[near_spec(near, other_side), table_spec(table, own_side)]
            + [ANYWHERE] * len(after),
            out_specs=fixed(shape),
        ),
        compiler_params=params(),
        cost_estimate=cost(3),
        name=name,
    )(half, near, table, *after)


def unfold_y(near_ref, far_ref, table, lines, store, kx_local):
    width = kx_local * 2 * MY
    groups = far_ref.shape[0]
    channels = groups * GROUP
    for g in range(0, groups, 2):
        pair = half_sums(near_ref, table, g, 2)
        for at in (g, g + 1):
            found = pair[:, (at - g) * LANES : (at - g + 1) * LANES] + far_ref[at]
            for part in range(2):
                lines[part, at * LANES : (at + 1) * LANES, :] = found[
                    part * width : (part + 1) * width, :
                ].T
    for part in range(2):
        for kz in range(MZ):
            piece = lines[part, pl.ds(kz, channels, stride=MZ), :]
            for j in range(kx_local):
                store(
                    part,
                    (j * MZ + kz) * 2 * MY,
                    piece[:, j * 2 * MY : (j + 1) * 2 * MY],
                )


def fold_modes(back, lines, send_ref, kx_local):
    channels = back.shape[1]
    for part in range(2):
        for kz in range(MZ):
            pieces = [
                back[part, :, (j * MZ + kz) * 2 * MY : (j * MZ + kz + 1) * 2 * MY]
                for j in range(kx_local)
            ]
            lines[part, pl.ds(kz, channels, stride=MZ), :] = jnp.concatenate(pieces, axis=1)
    width = kx_local * 2 * MY
    for g in range(channels // GROUP):
        for part in range(2):
            row = (2 * g + part) * width
            send_ref[row : row + width, :] = lines[part, g * LANES : (g + 1) * LANES, :].T


SUBLANES = 8


def spectrum_u(half_ref, near_ref, far_ref, table, skip_ref, *refs, kx_local):
    hat_ref, lines = refs[-2:]
    channels = skip_ref.shape[0]

    def store(part, column, values):
        hat_ref[part * channels : (part + 1) * channels, column : column + 2 * MY] = values

    unfold_y(near_ref, far_ref, table, lines, store, kx_local)
    hat_ref[2 * channels :, :] = jnp.zeros((SUBLANES, hat_ref.shape[1]), F32)
    for k in range(channels // SUBLANES):
        hat_ref[2 * channels :, k * LANES : (k + 1) * LANES] = skip_ref[
            k * SUBLANES : (k + 1) * SUBLANES, :
        ]


def finish_u(half, near, far, skip, kx_local, after=()):
    channels = far.shape[0] * GROUP
    table = y_forward_table(kx_local)
    shape = (2 * channels + SUBLANES, kx_local * MZ * 2 * MY)
    return pl.pallas_call(
        functools.partial(spectrum_u, kx_local=kx_local),
        out_shape=jax.ShapeDtypeStruct(shape, F32),
        grid_spec=pltpu.PrefetchScalarGridSpec(
            num_scalar_prefetch=1,
            grid=(1,),
            in_specs=[
                near_spec(near, own_side),
                fixed(far.shape),
                table_spec(table, own_side),
                fixed(skip.shape),
            ]
            + [ANYWHERE] * len(after),
            out_specs=fixed(shape),
            scratch_shapes=[pltpu.VMEM((2, channels * MZ, kx_local * 2 * MY), F32)],
        ),
        compiler_params=params(),
        cost_estimate=cost(4),
        name="finish_u",
    )(half, near, far, table, skip, *after)


def mode_scale(kz):
    return (1.0 if kz == 0 else 2.0) / float(NX * NY * NZ)


def through_weight(weight_ref, rounded, back, per_step, modes):
    step = pl.program_id(0)
    for start in range(0, modes, 128):
        lane = slice(start, start + 128)
        real = rounded[0, :, lane]
        imag = rounded[1, :, lane]
        reals, imags = [], []
        for i in range(per_step):
            weight_real = weight_ref[0, i, :, lane].astype(F32)
            weight_imag = weight_ref[1, i, :, lane].astype(F32)
            reals.append(
                jnp.sum(weight_real * real + weight_imag * imag, axis=0, keepdims=True)
            )
            imags.append(
                jnp.sum(weight_real * imag - weight_imag * real, axis=0, keepdims=True)
            )
        rows = pl.ds(pl.multiple_of(step * per_step, per_step), per_step)
        back[0, rows, lane] = jnp.concatenate(reals, axis=0)
        back[1, rows, lane] = jnp.concatenate(imags, axis=0)


def spectrum_e(half_ref, near_ref, far_ref, weight_ref, table, *refs, kx_local, per_step):
    hat_ref, rounded, send_ref, lines, back = refs[-5:]

    @pl.when(pl.program_id(0) == 0)
    def _():
        def store(part, column, values):
            hat_ref[part, :, column : column + 2 * MY] = values
            rounded[part, :, column : column + 2 * MY] = values.astype(BF16).astype(
                F32
            ) * mode_scale((column // (2 * MY)) % MZ)

        unfold_y(near_ref, far_ref, table, lines, store, kx_local)

    through_weight(weight_ref, rounded, back, per_step, kx_local * MZ * 2 * MY)

    @pl.when(pl.program_id(0) == pl.num_programs(0) - 1)
    def _():
        fold_modes(back, lines, send_ref, kx_local)


def spectrum_rest(rounded, weight_ref, skip_ref, send_ref, lines, back, *, kx_local, per_step):
    through_weight(weight_ref, rounded, back, per_step, kx_local * MZ * 2 * MY)

    @pl.when(pl.program_id(0) == pl.num_programs(0) - 1)
    def _():
        fold_modes(back, lines, send_ref, kx_local)
        skip = jnp.sum(skip_ref[...], axis=0)
        channels = rounded.shape[1]
        first = send_ref.shape[0] - channels
        for k in range(channels // SUBLANES):
            send_ref[first + k * SUBLANES : first + (k + 1) * SUBLANES, :] = skip[
                :, k * LANES : (k + 1) * LANES
            ]


def finish_e(half, near, far, weight, kx_local, after=()):
    channels = far.shape[0] * GROUP
    modes = kx_local * MZ * 2 * MY
    per_step = 8
    near_half = channels // 2
    table = y_forward_table(kx_local)
    spectrum = jax.ShapeDtypeStruct((2, channels, modes), F32)
    send = jax.ShapeDtypeStruct((far.shape[0] // 2 * far.shape[1], LANES), F32)
    return pl.pallas_call(
        functools.partial(spectrum_e, kx_local=kx_local, per_step=per_step),
        out_shape=(spectrum, spectrum, send),
        grid_spec=pltpu.PrefetchScalarGridSpec(
            num_scalar_prefetch=1,
            grid=(near_half // per_step,),
            in_specs=[
                near_spec(near, own_side),
                fixed(far.shape),
                pl.BlockSpec((2, per_step, channels, modes), lambda i, at: (0, i, 0, 0)),
                table_spec(table, own_side),
            ]
            + [ANYWHERE] * len(after),
            out_specs=(fixed(spectrum.shape), fixed(spectrum.shape), fixed(send.shape)),
            scratch_shapes=[
                pltpu.VMEM((2, channels * MZ, kx_local * 2 * MY), F32),
                pltpu.VMEM((2, near_half, modes), F32),
            ],
        ),
        compiler_params=params(),
        cost_estimate=cost(8),
        name="finish_e",
    )(half, near, far, weight, table, *after)


def finish_rest(rounded, weight, all_u, kx_local):
    _, channels, modes = rounded.shape
    per_step = 8
    rest = channels // 2
    steps = rest // per_step
    rows = rest // GROUP * 2 * kx_local * 2 * MY + channels
    skip_block = (all_u.shape[0], SUBLANES, channels // SUBLANES * LANES)
    send = jax.ShapeDtypeStruct((rows, LANES), F32)
    return pl.pallas_call(
        functools.partial(spectrum_rest, kx_local=kx_local, per_step=per_step),
        out_shape=send,
        grid=(steps,),
        in_specs=[
            whole(rounded.shape),
            pl.BlockSpec((2, per_step, channels, modes), lambda i: (0, i + steps, 0, 0)),
            pl.BlockSpec(skip_block, lambda i: (0, 2 * channels // SUBLANES, 0)),
        ],
        out_specs=whole(send.shape),
        scratch_shapes=[
            pltpu.VMEM((2, rest * MZ, kx_local * 2 * MY), F32),
            pltpu.VMEM((2, rest, modes), F32),
        ],
        compiler_params=params(),
        cost_estimate=cost(5),
        name="finish_rest",
    )(rounded, weight, all_u)


def expand_body(half_ref, own_ref, far_ref, table, *refs, groups):
    send_ref = refs[-1]
    relays = send_ref.shape[0]
    per_group = table.shape[1] // relays
    modes = table.shape[2] // 3
    half = half_ref[0]
    for ref, side in ((own_ref, half), (far_ref, 1 - half)):
        for g in range(0, groups, 2):
            data = jnp.concatenate(
                [ref[at * modes : (at + 1) * modes, :] for at in (g, g + 1)], axis=1
            )
            found = dot_split(table[0], data)
            for r in range(relays):
                for at in (g, g + 1):
                    send_ref[r, side, at * per_group : (at + 1) * per_group, :] = found[
                        r * per_group : (r + 1) * per_group,
                        (at - g) * LANES : (at - g + 1) * LANES,
                    ]
    left = own_ref.shape[0] - groups * modes
    if left:
        total = own_ref[groups * modes :, :] + far_ref[groups * modes :, :]
        for r in range(relays):
            send_ref[r, 0, groups * per_group :, :] = total
            send_ref[r, 1, groups * per_group :, :] = total


def expand(half, own, far, relays, groups, kx_local, after=()):
    table = y_inverse_table(kx_local)
    left = own.shape[0] - groups * table.shape[2] // 3
    shape = (relays, 2, groups * table.shape[1] // relays + left, LANES)
    return pl.pallas_call(
        functools.partial(expand_body, groups=groups),
        out_shape=jax.ShapeDtypeStruct(shape, F32),
        grid_spec=pltpu.PrefetchScalarGridSpec(
            num_scalar_prefetch=1,
            grid=(1,),
            in_specs=[fixed(own.shape), fixed(far.shape), table_spec(table, own_side)]
            + [ANYWHERE] * len(after),
            out_specs=fixed(shape),
        ),
        compiler_params=params(),
        cost_estimate=cost(4),
        name="expand",
    )(half, own, far, table, *after)


PLANES = 8


def mix_body(input_ref, cot_ref, weight_ref, *refs, planes, count):
    mixed_ref, skip_ref, total, spread = refs[-4:]
    step = pl.program_id(0)
    channels = input_ref.shape[0]
    side = channels * PLANES

    def pick(shape, axis):
        line = lax.broadcasted_iota(jnp.int32, shape, axis) // PLANES
        return line == lax.broadcasted_iota(jnp.int32, shape, 1 - axis)

    def same_plane():
        row = lax.broadcasted_iota(jnp.int32, (side, side), 0)
        column = lax.broadcasted_iota(jnp.int32, (side, side), 1)
        return row % PLANES == column % PLANES

    @pl.when(step == 0)
    def _():
        total[...] = jnp.zeros_like(total)
        tall = dot(pick((side, channels), 0).astype(BF16), weight_ref[...]).astype(BF16)
        wide = dot(tall, pick((channels, side), 1).astype(BF16))
        spread[...] = jnp.where(same_plane(), wide, 0.0).astype(BF16)

    mixed = [[] for _ in range(count)]
    for first in range(0, planes, PLANES):
        cots, lefts = [], []
        for k in range(count):
            rows = slice(k * planes, (k + 1) * planes)
            near = slice(first, first + PLANES)
            cots.append(cot_ref[:, rows, :].astype(F32)[:, near].reshape(side, NZ))
            lefts.append(input_ref[:, rows, :].astype(F32)[:, near].reshape(side, NZ))
        cot = jnp.concatenate(cots, axis=1).astype(BF16)
        left = jnp.concatenate(lefts, axis=1).astype(BF16)
        total[...] += lax.dot_general(
            left, cot, (((1,), (1,)), ((), ())), preferred_element_type=F32
        )
        found = dot(spread[...], cot)
        for k in range(count):
            mixed[k].append(found[:, k * NZ : (k + 1) * NZ].reshape(channels, PLANES, NZ))
    for k in range(count):
        mixed_ref[:, k * planes : (k + 1) * planes, :] = jnp.concatenate(
            mixed[k], axis=1
        ).astype(BF16)

    @pl.when(step == pl.num_programs(0) - 1)
    def _():
        kept = jnp.where(same_plane(), total[...], 0.0)
        half = lax.dot_general(
            kept,
            pick((side, LANES), 0).astype(F32),
            (((1,), (0,)), ((), ())),
            precision=lax.Precision.HIGHEST,
            preferred_element_type=F32,
        )
        skip_ref[...] = lax.dot_general(
            pick((channels, side), 1).astype(F32),
            half,
            (((1,), (0,)), ((), ())),
            precision=lax.Precision.HIGHEST,
            preferred_element_type=F32,
        )


def mix(inputs, cot, weight, planes, after=()):
    channels, rows, _ = inputs.shape
    count = 16
    side = channels * PLANES
    spec = pl.BlockSpec((channels, count * planes, NZ), lambda x: (0, x, 0))
    return pl.pallas_call(
        functools.partial(mix_body, planes=planes, count=count),
        out_shape=(
            jax.ShapeDtypeStruct(inputs.shape, BF16),
            jax.ShapeDtypeStruct((channels, LANES), F32),
        ),
        grid=(NX // count,),
        in_specs=[spec, spec, whole((channels, channels))] + [ANYWHERE] * len(after),
        out_specs=(spec, whole((channels, LANES))),
        scratch_shapes=[pltpu.VMEM((side, side), F32), pltpu.VMEM((side, side), BF16)],
        compiler_params=params(),
        cost_estimate=cost(22),
        name="mix",
    )(inputs, cot, weight, *after)


def x_then_z(
    received_ref, mixed_ref, table_x, table_z, out_ref, real_ref, imag_ref, planes, blocks
):
    relays = received_ref.shape[0]
    part = 2 * MX // relays
    rows = NX * planes // blocks
    block = pl.program_id(1)

    @pl.when(block == 0)
    def _():
        for y in range(0, planes, 2):
            pair = [
                jnp.concatenate(
                    [
                        received_ref[r, side, at * part : (at + 1) * part, :]
                        for side in range(2)
                        for r in range(relays)
                    ],
                    axis=0,
                ).astype(BF16)
                for at in (y, y + 1)
            ]
            found = dot(table_x[...], jnp.concatenate(pair, axis=1))
            for place in range(2):
                lane = slice(place * LANES, (place + 1) * LANES)
                real_ref[pl.ds(y + place, NX, stride=planes), :] = found[:NX, lane]
                imag_ref[pl.ds(y + place, NX, stride=planes), :] = found[NX:, lane]

    step = min(rows, 256)
    for start in range(0, rows, step):
        place = pl.ds(pl.multiple_of(block * rows + start, step), step)
        line = jnp.concatenate([real_ref[place, :], imag_ref[place, :]], axis=1).astype(BF16)
        found = dot(line, table_z[...])
        for c in range(GROUP):
            mixed = mixed_ref[c, start : start + step, :].astype(F32)
            out_ref[c, start : start + step, :] = (
                found[:, c * NZ : (c + 1) * NZ] + mixed
            ).astype(BF16)


def grid_plain(*refs, planes, blocks):
    x_then_z(*refs, planes, blocks)


def grid_skip(received_ref, skip_ref, *refs, planes, blocks, root):
    mixed_ref, table_x, table_z = refs[:3]
    out_ref, total_ref, real_ref, imag_ref = refs[-4:]

    @pl.when((pl.program_id(0) == 0) & (pl.program_id(1) == 0))
    def _():
        total = jnp.sum(skip_ref[:, 0], axis=0)
        total_ref[...] = total[:, : total_ref.shape[1]] / root

    x_then_z(
        received_ref, mixed_ref, table_x, table_z, out_ref, real_ref, imag_ref, planes, blocks
    )


def grid_of(received, mixed, first, groups, planes, root=None, after=()):
    relays, _, rows, _ = received.shape
    channels = mixed.shape[0]
    blocks = 1
    part = 2 * MX // relays
    per_group = planes * part
    spec = pl.BlockSpec((GROUP, NX * planes // blocks, NZ), lambda g, r: (g + first, r, 0))
    in_specs = [
        pl.BlockSpec((relays, 2, per_group, LANES), lambda g, r: (0, 0, g, 0)),
        spec,
        whole((2 * NX, 4 * MX)),
        whole((2 * LANES, GROUP * NZ)),
    ]
    operands = [received, mixed, x_inverse_table(2 * relays), z_inverse_table()]
    out_shape = (jax.ShapeDtypeStruct(mixed.shape, BF16),)
    out_specs = (spec,)
    body = functools.partial(grid_plain, planes=planes, blocks=blocks)
    if root is not None:
        extra = groups * per_group // channels
        in_specs.insert(1, pl.BlockSpec((relays, 1, channels, LANES), lambda g, r: (0, 0, extra, 0)))
        operands.insert(1, received)
        out_shape += (jax.ShapeDtypeStruct((channels, channels), F32),)
        out_specs += (whole((channels, channels)),)
        body = functools.partial(grid_skip, planes=planes, blocks=blocks, root=root)
    operands += after
    in_specs += [ANYWHERE] * len(after)
    return pl.pallas_call(
        body,
        out_shape=out_shape,
        grid=(groups, blocks),
        in_specs=in_specs,
        out_specs=out_specs,
        scratch_shapes=[
            pltpu.VMEM((NX * planes, LANES), F32),
            pltpu.VMEM((NX * planes, LANES), F32),
        ],
        input_output_aliases={1 if root is None else 2: 0},
        compiler_params=params(2),
        cost_estimate=cost(9),
        name="to_grid",
    )(*operands)


def cross_body(own_ref, left_ref, right_ref, *refs, samples):
    out_ref = refs[-1]
    lanes = out_ref.shape[-1]
    channels = left_ref.shape[1] // 2
    own = right_ref.shape[2]
    kz = lax.broadcasted_iota(jnp.int32, (own, lanes), 1) // (2 * MY) % MZ
    scale = jnp.where(kz == 0, 1.0, 2.0) / float(NX * NY * NZ)
    rights = [
        (right_ref[b, 0] * scale, right_ref[b, 1] * scale) for b in range(samples)
    ]
    for i in range(channels):
        real = imag = None
        for b in range(samples):
            left_real = left_ref[b, i : i + 1, :]
            left_imag = left_ref[b, channels + i : channels + i + 1, :]
            right_real, right_imag = rights[b]
            one = left_real * right_real + left_imag * right_imag
            two = left_real * right_imag - left_imag * right_real
            real = one if real is None else real + one
            imag = two if imag is None else imag + two
        out_ref[0, i] = real
        out_ref[1, i] = imag


def cross(left, right, place, own, after=()):
    samples, _, channels, modes = right.shape
    lanes = 2 * MY * MZ
    return pl.pallas_call(
        functools.partial(cross_body, samples=samples),
        out_shape=jax.ShapeDtypeStruct((2, channels, own, modes), F32),
        grid_spec=pltpu.PrefetchScalarGridSpec(
            num_scalar_prefetch=1,
            grid=(modes // lanes,),
            in_specs=[
                pl.BlockSpec((samples, 2 * channels, lanes), lambda k, at: (0, 0, k)),
                pl.BlockSpec((samples, 2, own, lanes), lambda k, at: (0, 0, at[0], k)),
            ]
            + [ANYWHERE] * len(after),
            out_specs=pl.BlockSpec((2, channels, own, lanes), lambda k, at: (0, 0, 0, k)),
        ),
        compiler_params=params(),
        cost_estimate=cost(6),
        name="cross",
    )(place, left, right, *after)


def exchange_near(values):
    spaces = lax.axis_size("space")
    groups = [list(range(spaces // 2)), list(range(spaces // 2, spaces))]
    return lax.all_to_all(
        values, "space", split_axis=0, concat_axis=0, axis_index_groups=groups, tiled=True
    )


def exchange_far(values, turned=False):
    spaces = lax.axis_size("space")
    pairs = [(s, (s + spaces // 2) % spaces) for s in range(spaces)]
    pairs = pairs[::-1] if turned else pairs
    return lax.ppermute(values, "space", pairs)


HIGHEST = lax.Precision.HIGHEST


def phase_table(length, count, signed):
    points = jnp.arange(length, dtype=jnp.int32)
    orders = jnp.arange(count, dtype=jnp.int32)
    if signed:
        orders = jnp.where(orders < count // 2, orders, orders - count)
    residues = jnp.mod(points[:, None] * orders[None, :], length)
    radians = residues.astype(jnp.float32) * (2.0 * math.pi / length)
    return (jnp.cos(radians), jnp.sin(radians))


def forward_block(cosine, sine):
    return jnp.stack(
        [jnp.stack([cosine, -sine], axis=1), jnp.stack([sine, cosine], axis=1)], axis=0
    )


def inverse_block(cosine, sine):
    cos_rows = cosine.T
    sin_rows = sine.T
    return jnp.stack(
        [jnp.stack([cos_rows, sin_rows], axis=1), jnp.stack([-sin_rows, cos_rows], axis=1)], axis=0
    )


def local_spectrum(grid_in):
    cos_x, sin_x = phase_table(NX, 2 * MX, True)
    table_x = jnp.stack([cos_x, -sin_x], axis=1).astype(jnp.bfloat16)
    section_x = jnp.einsum(
        "scxyz,xpa->scpayz", grid_in, table_x, preferred_element_type=jnp.float32
    )
    cos_z, sin_z = phase_table(NZ, MZ, False)
    section_z = jnp.einsum(
        "scpayz,pzqk->scqyak", section_x, forward_block(cos_z, sin_z), precision=HIGHEST
    )
    return section_z.reshape(
        section_z.shape[0], section_z.shape[1], 2, section_z.shape[3], 2 * MX * MZ
    )


def along_y(spectra):
    cos_y, sin_y = phase_table(NY, 2 * MY, True)
    section_y = jnp.einsum(
        "scpym,pyqk->scqmk", spectra, forward_block(cos_y, sin_y), precision=HIGHEST
    )
    return section_y.reshape(section_y.shape[0], section_y.shape[1], 2, section_y.shape[3] * 2 * MY)


def both_along_y(spectra_pair):
    return (along_y(spectra_pair[0]), along_y(spectra_pair[1]))


def to_grid(spectra):
    shaped = spectra.reshape(spectra.shape[0], spectra.shape[1], 2, spectra.shape[3], 2 * MX, MZ)
    cos_z, sin_z = phase_table(NZ, MZ, False)
    grid_z = jnp.einsum(
        "scpyak,pkqz->scqayz", shaped, inverse_block(cos_z, sin_z), precision=HIGHEST
    )
    cos_x, sin_x = phase_table(NX, 2 * MX, True)
    table_x = jnp.stack([cos_x.T, -sin_x.T], axis=0)
    return jnp.einsum("scpayz,pax->scxyz", grid_z, table_x, precision=HIGHEST)


def cross_terms(spec_left, spec_right):
    real_part = jnp.einsum(
        "sim,som->iom", spec_left[:, :, 0], spec_right[:, :, 0], precision=HIGHEST
    )
    real_part = real_part + jnp.einsum(
        "sim,som->iom", spec_left[:, :, 1], spec_right[:, :, 1], precision=HIGHEST
    )
    imag_part = jnp.einsum(
        "sim,som->iom", spec_left[:, :, 0], spec_right[:, :, 1], precision=HIGHEST
    )
    imag_part = imag_part - jnp.einsum(
        "sim,som->iom", spec_left[:, :, 1], spec_right[:, :, 0], precision=HIGHEST
    )
    return jnp.stack([real_part, imag_part], axis=0)


def contract(weight_part, spec_part):
    return jnp.einsum("iom,som->sim", weight_part, spec_part, preferred_element_type=jnp.float32)


def skip_gradient(grid_in, cot_pre):
    partial_sum = jnp.einsum(
        "sixyz,soxyz->io", grid_in, cot_pre, preferred_element_type=jnp.float32
    )
    summed = lax.psum(partial_sum, ("batch", "space"))
    return summed / math.sqrt(grid_in.shape[0] * lax.axis_size("batch") * NX * NY * NZ)


def general(inputs, pre_act, cotangent, spectral_weight, skip_weight):
    samples = inputs.shape[0]
    channels = inputs.shape[1]
    slope_pre = slope(pre_act.astype(jnp.float32))
    cot_pre = (cotangent.astype(jnp.float32) * slope_pre).astype(jnp.bfloat16)
    spec_u, spec_e = both_along_y(
        (
            lax.all_to_all(
                local_spectrum(inputs), "space", split_axis=4, concat_axis=3, tiled=True
            ),
            lax.all_to_all(
                local_spectrum(cot_pre), "space", split_axis=4, concat_axis=3, tiled=True
            ),
        )
    )
    mode_count = spec_u.shape[3]
    position = jnp.arange(mode_count, dtype=jnp.int32)
    kxz_index = lax.axis_index("space") * (mode_count // (2 * MY)) + position // (2 * MY)
    mode_weights = jnp.where(kxz_index % MZ == 0, 1.0, 2.0).astype(jnp.float32) / float(
        NX * NY * NZ
    )
    mode_grad = lax.psum_scatter(
        cross_terms(spec_u, spec_e), "batch", scatter_dimension=2, tiled=True
    )
    grad_spectral = mode_grad * mode_weights
    rounded = spec_e.astype(jnp.bfloat16)
    weight_real = spectral_weight[0]
    weight_imag = spectral_weight[1]
    back_real = contract(weight_real, rounded[:, :, 0]) + contract(weight_imag, rounded[:, :, 1])
    back_imag = contract(weight_real, rounded[:, :, 1]) - contract(weight_imag, rounded[:, :, 0])
    back_modes = jnp.stack([back_real, back_imag], axis=2) * mode_weights
    shaped = back_modes.reshape(samples, channels, 2, mode_count // (2 * MY), 2 * MY)
    cos_y, sin_y = phase_table(NY, 2 * MY, True)
    grid_y = jnp.einsum("scpmk,pkqy->scqym", shaped, inverse_block(cos_y, sin_y), precision=HIGHEST)
    spatial = to_grid(lax.all_to_all(grid_y, "space", split_axis=3, concat_axis=4, tiled=True))
    mixed = jnp.einsum("io,soxyz->sixyz", skip_weight, cot_pre, preferred_element_type=jnp.float32)
    grad_inputs = (spatial + mixed).astype(jnp.bfloat16)
    grad_skip = skip_gradient(inputs, cot_pre)
    return (grad_inputs, grad_spectral, grad_skip)


def on_device(inputs, pre_act, cotangent, spectral_weight, skip_weight):
    samples, channels, _, planes, _ = inputs.shape
    spaces = lax.axis_size("space")
    batches = lax.axis_size("batch")
    if samples != 1 or spaces % 2 or (2 * MX) % spaces or planes % 16 or channels % (4 * GROUP):
        return general(inputs, pre_act, cotangent, spectral_weight, skip_weight)
    kx_local = 2 * MX // spaces
    flat = (channels, NX * planes, NZ)
    groups = channels // GROUP
    inputs, pre_act, cotangent = (v.reshape(flat) for v in (inputs, pre_act, cotangent))
    half = (lax.axis_index("space") // (spaces // 2)).astype(jnp.int32).reshape(1)
    batch = lax.axis_index("batch").astype(jnp.int32).reshape(1)
    middle = groups // 2
    (send_u,) = forward((inputs,), 0, groups, planes, spaces, False)
    near_u = exchange_near(send_u)
    send_e, cot_pre = forward(
        (pre_act, cotangent), 0, groups, planes, spaces, True, after=(send_u,)
    )
    near_e = exchange_near(send_e)
    part_u = partial_sums(half, near_u, groups, kx_local, "partial_u", after=(send_e,))
    far_u = exchange_far(part_u)
    mixed, skip_part = mix(inputs, cot_pre, skip_weight, planes, after=(part_u,))
    hat_u = finish_u(half, near_u, far_u, skip_part, kx_local)
    all_u = lax.all_gather(hat_u, "batch")
    part_e = partial_sums(half, near_e, groups, kx_local, "partial_e", after=(hat_u,))
    far_e = exchange_far(part_e)
    hat_e, rounded, modes_a = finish_e(
        half, near_e, far_e, spectral_weight, kx_local, after=(hat_u,)
    )
    far_a = exchange_far(modes_a)
    all_e = lax.all_gather(hat_e, "batch")
    modes_b = finish_rest(rounded, spectral_weight, all_u, kx_local)
    far_b = exchange_far(modes_b, turned=True)
    send_a = expand(half, modes_a, far_a, spaces // 2, middle, kx_local, after=(modes_b,))
    near_a = exchange_near(send_a)
    send_b = expand(half, modes_b, far_b, spaces // 2, middle, kx_local, after=(send_a,))
    near_b = exchange_near(send_b)
    grad_spectral = cross(all_u, all_e, batch, channels // batches, after=(send_b,))
    (grad_inputs,) = grid_of(near_a, mixed, 0, middle, planes)
    root = math.sqrt(samples * batches * NX * NY * NZ)
    grad_inputs, grad_skip = grid_of(near_b, grad_inputs, middle, middle, planes, root, (grad_spectral,))
    return (
        grad_inputs.reshape(samples, channels, NX, planes, NZ),
        grad_spectral,
        grad_skip,
    )


def solution(mesh):
    placed = (
        P("batch", None, None, "space", None),
        P("batch", None, None, "space", None),
        P("batch", None, None, "space", None),
        P(None, None, None, "space"),
        P(),
    )
    return jax.shard_map(
        on_device,
        mesh=mesh,
        in_specs=placed,
        out_specs=(P("batch", None, None, "space", None), P(None, None, "batch", "space"), P()),
        check_vma=False,
    )
```

```python
import functools
import math

import jax
import jax.numpy as jnp
import ml_dtypes
import numpy as np
from jax import lax
from jax.experimental import pallas as pl
from jax.experimental.pallas import tpu as pltpu
from jax.sharding import PartitionSpec as P

NX = 128
NY = 128
NZ = 128
MX = 16
MY = 16
MZ = 16
GROUP = 8
LANES = GROUP * MZ
BF16 = jnp.bfloat16
F32 = jnp.float32
VMEM_LIMIT = 62 * 1024 * 1024


def cost(microseconds):
    return pl.CostEstimate(flops=int(microseconds * 2e9), bytes_accessed=1, transcendentals=0)


def waves(length, count, signed):
    points = np.arange(length)
    orders = np.arange(count)
    if signed:
        orders = np.where(orders < count // 2, orders, orders - count)
    radians = np.mod(points[:, None] * orders[None, :], length) * (2.0 * math.pi / length)
    return np.cos(radians), np.sin(radians)


def rounded_table(table):
    return np.asarray(table, np.float32).astype(ml_dtypes.bfloat16)


def z_forward_table():
    cos, sin = waves(NZ, MZ, False)
    table = np.zeros((GROUP, NZ, 2, GROUP, MZ))
    for c in range(GROUP):
        table[c, :, 0, c, :] = cos
        table[c, :, 1, c, :] = -sin
    return jnp.asarray(rounded_table(table.reshape(GROUP * NZ, 2 * LANES)))


def z_inverse_table():
    cos, sin = waves(NZ, MZ, False)
    table = np.zeros((2, GROUP, MZ, GROUP, NZ))
    for c in range(GROUP):
        table[0, c, :, c, :] = cos.T
        table[1, c, :, c, :] = -sin.T
    return jnp.asarray(rounded_table(table.reshape(2 * LANES, GROUP * NZ)))


def x_forward_table(spaces):
    cos, sin = waves(NX, 2 * MX, True)
    cos = cos.T.reshape(spaces, 2 * MX // spaces, NX)
    sin = sin.T.reshape(spaces, 2 * MX // spaces, NX)
    table = np.stack([np.stack([cos, sin], axis=2), np.stack([-sin, cos], axis=2)], axis=1)
    return jnp.asarray(rounded_table(table.reshape(4 * MX, 2 * NX)))


def x_inverse_table(relays):
    cos, sin = waves(NX, 2 * MX, True)
    cos = cos.reshape(NX, 2, relays, MX // relays)
    sin = sin.reshape(NX, 2, relays, MX // relays)
    table = np.stack([np.stack([cos, -sin], axis=3), np.stack([sin, cos], axis=3)], axis=0)
    place = np.arange(relays)
    table = np.stack([table[:, :, :, place ^ r] for r in range(relays)])
    return jnp.asarray(rounded_table(table.reshape(relays, 2 * NX, 4 * MX)))


def split_table(table):
    high = rounded_table(table)
    low = rounded_table(table - high.astype(np.float64))
    return jnp.asarray(np.concatenate([high, high, low], axis=-1))


def y_forward_table(kx_local):
    cos, sin = waves(NY, 2 * MY, True)
    table = np.zeros((2, kx_local, 2 * MY, NY, 2, kx_local))
    for j in range(kx_local):
        table[0, j, :, :, 0, j] = cos.T
        table[0, j, :, :, 1, j] = sin.T
        table[1, j, :, :, 0, j] = -sin.T
        table[1, j, :, :, 1, j] = cos.T
    table = table.reshape(4 * MY * kx_local, 2, NY * kx_local)
    return split_table(table.swapaxes(0, 1))


def y_inverse_table(kx_local):
    cos, sin = waves(NY, 2 * MY, True)
    table = np.zeros((NY, 2, kx_local, 2, kx_local, 2 * MY))
    for j in range(kx_local):
        table[:, 0, j, 0, j, :] = cos
        table[:, 0, j, 1, j, :] = -sin
        table[:, 1, j, 0, j, :] = sin
        table[:, 1, j, 1, j, :] = cos
    return split_table(table.reshape(2, NY * kx_local, 4 * MY * kx_local))


def dot(left, right):
    return lax.dot_general(left, right, (((1,), (0,)), ((), ())), preferred_element_type=F32)


def dot_split(table, values):
    high = values.astype(BF16)
    low = (values - high.astype(F32)).astype(BF16)
    return dot(table, jnp.concatenate([high, low, high], axis=0))


def params(count=1):
    return pltpu.CompilerParams(
        vmem_limit_bytes=VMEM_LIMIT, dimension_semantics=("arbitrary",) * count
    )


def z_then_x(load, table_z, table_x, send_ref, real_ref, imag_ref, planes, spaces, blocks):
    rows = NX * planes // blocks
    block = pl.program_id(1)
    step = min(rows, 512)
    for start in range(0, rows, step):
        line = jnp.concatenate([load(c, start, step) for c in range(GROUP)], axis=1)
        found = dot(line, table_z[...])
        place = pl.ds(pl.multiple_of(block * rows + start, step), step)
        real_ref[place, :] = found[:, :LANES]
        imag_ref[place, :] = found[:, LANES:]
    part = 4 * MX // spaces

    @pl.when(block == blocks - 1)
    def _():
        for y in range(0, planes, 2):
            pair = []
            for at in (y, y + 1):
                real = real_ref[pl.ds(at, NX, stride=planes), :]
                imag = imag_ref[pl.ds(at, NX, stride=planes), :]
                pair.append(jnp.concatenate([real, imag], axis=0).astype(BF16))
            found = dot(table_x[...], jnp.concatenate(pair, axis=1))
            for place in range(2):
                for s in range(spaces):
                    relay, side = s % (spaces // 2), s // (spaces // 2)
                    rows_of = slice((y + place) * part, (y + place + 1) * part)
                    send_ref[relay, side, rows_of, :] = found[
                        s * part : (s + 1) * part, place * LANES : (place + 1) * LANES
                    ]


def forward_plain(
    field_ref, table_z, table_x, *refs, planes, spaces, blocks
):
    send_ref, real_ref, imag_ref = refs[-3:]

    def load(c, start, step):
        return field_ref[c, start : start + step, :]

    z_then_x(load, table_z, table_x, send_ref, real_ref, imag_ref, planes, spaces, blocks)


def slope(values):
    normal_cdf = 0.5 * (1.0 + lax.erf(values * (1.0 / math.sqrt(2.0))))
    density = jnp.exp(-0.5 * values * values) * (1.0 / math.sqrt(2.0 * math.pi))
    return normal_cdf + values * density


def forward_cot(pre_ref, cot_ref, table_z, table_x, *refs, planes, spaces, blocks):
    send_ref, out_ref, real_ref, imag_ref = refs[-4:]

    def load(c, start, step):
        pre = pre_ref[c, start : start + step, :].astype(F32)
        cot = cot_ref[c, start : start + step, :].astype(F32)
        made = (cot * slope(pre)).astype(BF16)
        out_ref[c, start : start + step, :] = made
        return made

    z_then_x(load, table_z, table_x, send_ref, real_ref, imag_ref, planes, spaces, blocks)


def whole(shape):
    return pl.BlockSpec(shape, lambda *_: (0,) * len(shape))


ANYWHERE = pl.BlockSpec(memory_space=pl.ANY)


def forward(fields, first, groups, planes, spaces, cot, after=()):
    channels, rows, _ = fields[0].shape
    blocks = 1
    part = 4 * MX // spaces
    field_spec = pl.BlockSpec((GROUP, rows // blocks, NZ), lambda g, r: (g + first, r, 0))
    send_shape = jax.ShapeDtypeStruct((spaces // 2, 2, groups * planes * part, LANES), F32)
    send_spec = pl.BlockSpec((spaces // 2, 2, planes * part, LANES), lambda g, r: (0, 0, g, 0))
    out_shape, out_specs = (send_shape,), (send_spec,)
    if cot:
        out_shape += (jax.ShapeDtypeStruct(fields[0].shape, BF16),)
        out_specs += (field_spec,)
    body = forward_cot if cot else forward_plain
    return pl.pallas_call(
        functools.partial(body, planes=planes, spaces=spaces, blocks=blocks),
        out_shape=out_shape,
        grid=(groups, blocks),
        in_specs=[field_spec] * len(fields)
        + [whole((GROUP * NZ, 2 * LANES)), whole((4 * MX, 2 * NX))]
        + [ANYWHERE] * len(after),
        out_specs=out_specs,
        scratch_shapes=[pltpu.VMEM((rows, LANES), F32), pltpu.VMEM((rows, LANES), F32)],
        compiler_params=params(2),
        cost_estimate=cost(25 if cot else 11),
        name="forward_e" if cot else "forward_u",
    )(*fields, z_forward_table(), x_forward_table(spaces), *after)


def half_sums(near_ref, table, g, count):
    relays = near_ref.shape[0]
    per_group = table.shape[2] // 3 // relays
    data = jnp.concatenate(
        [
            jnp.concatenate(
                [
                    near_ref[r, 0, at * per_group : (at + 1) * per_group, :]
                    for at in range(g, g + count)
                ],
                axis=1,
            )
            for r in range(relays)
        ],
        axis=0,
    )
    return dot_split(table[0], data)


def partial_body(half_ref, near_ref, table, *refs, groups, riding):
    out_ref = refs[-1]
    rows = table.shape[1]
    for g in range(0, groups, 2):
        found = half_sums(near_ref, table, g, 2)
        out_ref[g * rows : (g + 1) * rows, :] = found[:, :LANES]
        out_ref[(g + 1) * rows : (g + 2) * rows, :] = found[:, LANES:]
    if riding:
        out_ref[groups * rows :, :] = refs[0][...]


def table_spec(table, side):
    return pl.BlockSpec((1,) + table.shape[1:], lambda *at: (side(at[-1][0]), 0, 0))


def near_spec(near, side):
    shape = (near.shape[0], 1) + near.shape[2:]
    return pl.BlockSpec(shape, lambda *at: (0, side(at[-1][0]), 0, 0))


def own_side(half):
    return half


def other_side(half):
    return 1 - half


def fixed(shape):
    return pl.BlockSpec(shape, lambda *at: (0,) * len(shape))


def partial_sums(half, near, groups, kx_local, name, riding=(), after=()):
    table = y_forward_table(kx_local)
    rows = groups * table.shape[1] + sum(v.shape[0] for v in riding)
    return pl.pallas_call(
        functools.partial(partial_body, groups=groups, riding=bool(riding)),
        out_shape=jax.ShapeDtypeStruct((rows, LANES), F32),
        grid_spec=pltpu.PrefetchScalarGridSpec(
            num_scalar_prefetch=1,
            grid=(1,),
            in_specs=[near_spec(near, other_side), table_spec(table, own_side)]
            + [fixed(v.shape) for v in riding]
            + [ANYWHERE] * len(after),
            out_specs=fixed((rows, LANES)),
        ),
        compiler_params=params(),
        cost_estimate=cost(3),
        name=name,
    )(half, near, table, *riding, *after)


def unfold_y(near_ref, far_ref, table, lines, store, kx_local):
    width = kx_local * 2 * MY
    channels = lines.shape[1] // MZ
    groups = channels // GROUP
    for g in range(0, groups, 2):
        pair = half_sums(near_ref, table, g, 2)
        for at in (g, g + 1):
            found = pair[:, (at - g) * LANES : (at - g + 1) * LANES] + far_ref[
                2 * at * width : 2 * (at + 1) * width, :
            ]
            for part in range(2):
                lines[part, at * LANES : (at + 1) * LANES, :] = found[
                    part * width : (part + 1) * width, :
                ].T
    for part in range(2):
        for kz in range(MZ):
            piece = lines[part, pl.ds(kz, channels, stride=MZ), :]
            for j in range(kx_local):
                store(
                    part,
                    (j * MZ + kz) * 2 * MY,
                    piece[:, j * 2 * MY : (j + 1) * 2 * MY],
                )


def fold_modes(back, lines, send_ref, kx_local):
    channels = back.shape[1]
    for part in range(2):
        for kz in range(MZ):
            pieces = [
                back[part, :, (j * MZ + kz) * 2 * MY : (j * MZ + kz + 1) * 2 * MY]
                for j in range(kx_local)
            ]
            lines[part, pl.ds(kz, channels, stride=MZ), :] = jnp.concatenate(pieces, axis=1)
    width = kx_local * 2 * MY
    for g in range(channels // GROUP):
        for part in range(2):
            row = (2 * g + part) * width
            send_ref[row : row + width, :] = lines[part, g * LANES : (g + 1) * LANES, :].T


SUBLANES = 8


def spectrum_u(half_ref, near_ref, far_ref, table, *refs, kx_local):
    hat_ref, lines = refs[-2:]
    channels = hat_ref.shape[0] // 2

    def store(part, column, values):
        hat_ref[part * channels : (part + 1) * channels, column : column + 2 * MY] = values

    unfold_y(near_ref, far_ref, table, lines, store, kx_local)


def finish_u(half, near, far, channels, kx_local, after=()):
    table = y_forward_table(kx_local)
    shape = (2 * channels, kx_local * MZ * 2 * MY)
    return pl.pallas_call(
        functools.partial(spectrum_u, kx_local=kx_local),
        out_shape=jax.ShapeDtypeStruct(shape, F32),
        grid_spec=pltpu.PrefetchScalarGridSpec(
            num_scalar_prefetch=1,
            grid=(1,),
            in_specs=[near_spec(near, own_side), fixed(far.shape), table_spec(table, own_side)]
            + [ANYWHERE] * len(after),
            out_specs=fixed(shape),
            scratch_shapes=[pltpu.VMEM((2, channels * MZ, kx_local * 2 * MY), F32)],
        ),
        compiler_params=params(),
        cost_estimate=cost(4),
        name="finish_u",
    )(half, near, far, table, *after)


def mode_scale(kz):
    return (1.0 if kz == 0 else 2.0) / float(NX * NY * NZ)


def through_weight(weight_ref, rounded, back, per_step, modes):
    step = pl.program_id(0)
    for start in range(0, modes, 128):
        lane = slice(start, start + 128)
        real = rounded[0, :, lane]
        imag = rounded[1, :, lane]
        reals, imags = [], []
        for i in range(per_step):
            weight_real = weight_ref[0, i, :, lane].astype(F32)
            weight_imag = weight_ref[1, i, :, lane].astype(F32)
            reals.append(
                jnp.sum(weight_real * real + weight_imag * imag, axis=0, keepdims=True)
            )
            imags.append(
                jnp.sum(weight_real * imag - weight_imag * real, axis=0, keepdims=True)
            )
        rows = pl.ds(pl.multiple_of(step * per_step, per_step), per_step)
        back[0, rows, lane] = jnp.concatenate(reals, axis=0)
        back[1, rows, lane] = jnp.concatenate(imags, axis=0)


def spectrum_e(
    batch_ref,
    half_ref,
    near_ref,
    far_ref,
    weight_ref,
    table,
    skip_ref,
    *refs,
    kx_local,
    per_step,
    batches,
):
    rounded, send_ref, hat, lines, back = refs[-5:]
    own_refs = refs[-5 - batches : -5]
    channels = skip_ref.shape[0]
    own = channels // batches

    @pl.when(pl.program_id(0) == 0)
    def _():
        def store(part, column, values):
            hat[part, :, column : column + 2 * MY] = values
            rounded[part, :, column : column + 2 * MY] = values.astype(BF16).astype(
                F32
            ) * mode_scale((column // (2 * MY)) % MZ)

        unfold_y(near_ref, far_ref, table, lines, store, kx_local)
        skip = skip_ref[...] + far_ref[far_ref.shape[0] - channels :, :]
        for d in range(batches):
            first = jnp.bitwise_xor(batch_ref[0], d) * own
            rows = pl.ds(pl.multiple_of(first, own), own)
            own_refs[d][:own, :] = hat[0, rows, :]
            own_refs[d][own : 2 * own, :] = hat[1, rows, :]
            own_refs[d][2 * own :, :] = jnp.zeros((SUBLANES, hat.shape[2]), F32)
            for k in range(channels // SUBLANES):
                own_refs[d][2 * own :, k * LANES : (k + 1) * LANES] = skip[
                    k * SUBLANES : (k + 1) * SUBLANES, :
                ]

    through_weight(weight_ref, rounded, back, per_step, kx_local * MZ * 2 * MY)

    @pl.when(pl.program_id(0) == pl.num_programs(0) - 1)
    def _():
        fold_modes(back, lines, send_ref, kx_local)


def spectrum_rest(rounded, weight_ref, *refs, kx_local, per_step):
    send_ref, lines, back = refs[-3:]
    through_weight(weight_ref, rounded, back, per_step, kx_local * MZ * 2 * MY)

    @pl.when(pl.program_id(0) == pl.num_programs(0) - 1)
    def _():
        fold_modes(back, lines, send_ref, kx_local)


def finish_e(batch, half, near, far, weight, skip, kx_local, batches, after=()):
    channels = skip.shape[0]
    modes = kx_local * MZ * 2 * MY
    per_step = 8
    near_half = channels // 2
    table = y_forward_table(kx_local)
    own = jax.ShapeDtypeStruct((2 * channels // batches + SUBLANES, modes), F32)
    spectrum = jax.ShapeDtypeStruct((2, channels, modes), F32)
    send = jax.ShapeDtypeStruct((near_half // GROUP * 2 * kx_local * 2 * MY, LANES), F32)
    *owns, rounded, sent = pl.pallas_call(
        functools.partial(spectrum_e, kx_local=kx_local, per_step=per_step, batches=batches),
        out_shape=(own,) * batches + (spectrum, send),
        grid_spec=pltpu.PrefetchScalarGridSpec(
            num_scalar_prefetch=2,
            grid=(near_half // per_step,),
            in_specs=[
                near_spec(near, own_side),
                fixed(far.shape),
                pl.BlockSpec((2, per_step, channels, modes), lambda i, *at: (0, i, 0, 0)),
                table_spec(table, own_side),
                fixed(skip.shape),
            ]
            + [ANYWHERE] * len(after),
            out_specs=(fixed(own.shape),) * batches + (fixed(spectrum.shape), fixed(send.shape)),
            scratch_shapes=[
                pltpu.VMEM((2, channels, modes), F32),
                pltpu.VMEM((2, channels * MZ, kx_local * 2 * MY), F32),
                pltpu.VMEM((2, near_half, modes), F32),
            ],
        ),
        compiler_params=params(),
        cost_estimate=cost(8),
        name="finish_e",
    )(batch, half, near, far, weight, table, skip, *after)
    return owns, rounded, sent


def finish_rest(rounded, weight, kx_local, after=()):
    _, channels, modes = rounded.shape
    per_step = 8
    rest = channels // 2
    steps = rest // per_step
    send = jax.ShapeDtypeStruct((rest // GROUP * 2 * kx_local * 2 * MY, LANES), F32)
    return pl.pallas_call(
        functools.partial(spectrum_rest, kx_local=kx_local, per_step=per_step),
        out_shape=send,
        grid=(steps,),
        in_specs=[
            whole(rounded.shape),
            pl.BlockSpec((2, per_step, channels, modes), lambda i: (0, i + steps, 0, 0)),
        ]
        + [ANYWHERE] * len(after),
        out_specs=whole(send.shape),
        scratch_shapes=[
            pltpu.VMEM((2, rest * MZ, kx_local * 2 * MY), F32),
            pltpu.VMEM((2, rest, modes), F32),
        ],
        compiler_params=params(),
        cost_estimate=cost(5),
        name="finish_rest",
    )(rounded, weight, *after)


def expand_body(
    half_ref, relay_ref, own_ref, far_ref, table, *refs, groups, channels, relays, riding
):
    send_refs = refs[-relays - 1 : -1]
    lines = refs[-1]
    per_group = table.shape[1] // relays
    modes = table.shape[2] // 3
    half = half_ref[0]
    at_line = 0
    for ref, side in ((own_ref, half), (far_ref, 1 - half)):
        for g in range(0, groups, 2):
            data = jnp.concatenate(
                [ref[at * modes : (at + 1) * modes, :] for at in (g, g + 1)], axis=1
            )
            lines[at_line] = dot_split(table[0], data)
            for d in range(relays):
                place = jnp.bitwise_xor(relay_ref[0], d) * per_group
                rows = pl.ds(pl.multiple_of(place, per_group), per_group)
                for at in (g, g + 1):
                    send_refs[d][side, at * per_group : (at + 1) * per_group, :] = lines[
                        at_line, rows, (at - g) * LANES : (at - g + 1) * LANES
                    ]
            at_line += 1
    if channels:
        skip = sum(ref[...] for ref in refs[:riding])
        for d in range(relays):
            for side in range(2):
                for k in range(channels // SUBLANES):
                    row = groups * per_group + k * SUBLANES
                    send_refs[d][side, row : row + SUBLANES, :] = skip[
                        :, k * LANES : (k + 1) * LANES
                    ]


def expand(half, relay, own, far, relays, groups, kx_local, riding=(), channels=0, after=()):
    table = y_inverse_table(kx_local)
    shape = (2, groups * table.shape[1] // relays + channels, LANES)
    skip_specs = [
        pl.BlockSpec(
            (SUBLANES, channels // SUBLANES * LANES),
            lambda *at: (riding[0].shape[0] // SUBLANES - 1, 0),
        )
        for _ in riding
    ]
    return pl.pallas_call(
        functools.partial(
            expand_body, groups=groups, channels=channels, relays=relays, riding=len(riding)
        ),
        out_shape=(jax.ShapeDtypeStruct(shape, F32),) * relays,
        grid_spec=pltpu.PrefetchScalarGridSpec(
            num_scalar_prefetch=2,
            grid=(1,),
            in_specs=[
                fixed(own.shape),
                fixed(far.shape),
                pl.BlockSpec((1,) + table.shape[1:], lambda i, half, relay: (half[0], 0, 0)),
            ]
            + skip_specs
            + [ANYWHERE] * len(after),
            out_specs=(fixed(shape),) * relays,
            scratch_shapes=[pltpu.VMEM((groups, table.shape[1], 2 * LANES), F32)],
        ),
        compiler_params=params(),
        cost_estimate=cost(60),
        name="expand",
    )(half, relay, own, far, table, *riding, *after)


PLANES = 8


def mix_body(input_ref, cot_ref, weight_ref, *refs, planes, count):
    mixed_ref, skip_ref, total, spread = refs[-4:]
    step = pl.program_id(0)
    channels = input_ref.shape[0]
    side = channels * PLANES

    def pick(shape, axis):
        line = lax.broadcasted_iota(jnp.int32, shape, axis) // PLANES
        return line == lax.broadcasted_iota(jnp.int32, shape, 1 - axis)

    def same_plane():
        row = lax.broadcasted_iota(jnp.int32, (side, side), 0)
        column = lax.broadcasted_iota(jnp.int32, (side, side), 1)
        return row % PLANES == column % PLANES

    @pl.when(step == 0)
    def _():
        total[...] = jnp.zeros_like(total)
        tall = dot(pick((side, channels), 0).astype(BF16), weight_ref[...]).astype(BF16)
        wide = dot(tall, pick((channels, side), 1).astype(BF16))
        spread[...] = jnp.where(same_plane(), wide, 0.0).astype(BF16)

    mixed = [[] for _ in range(count)]
    for first in range(0, planes, PLANES):
        cots, lefts = [], []
        for k in range(count):
            rows = slice(k * planes, (k + 1) * planes)
            near = slice(first, first + PLANES)
            cots.append(cot_ref[:, rows, :].astype(F32)[:, near].reshape(side, NZ))
            lefts.append(input_ref[:, rows, :].astype(F32)[:, near].reshape(side, NZ))
        cot = jnp.concatenate(cots, axis=1).astype(BF16)
        left = jnp.concatenate(lefts, axis=1).astype(BF16)
        total[...] += lax.dot_general(
            left, cot, (((1,), (1,)), ((), ())), preferred_element_type=F32
        )
        found = dot(spread[...], cot)
        for k in range(count):
            mixed[k].append(found[:, k * NZ : (k + 1) * NZ].reshape(channels, PLANES, NZ))
    for k in range(count):
        mixed_ref[:, k * planes : (k + 1) * planes, :] = jnp.concatenate(
            mixed[k], axis=1
        ).astype(BF16)

    @pl.when(step == pl.num_programs(0) - 1)
    def _():
        kept = jnp.where(same_plane(), total[...], 0.0)
        half = lax.dot_general(
            kept,
            pick((side, LANES), 0).astype(F32),
            (((1,), (0,)), ((), ())),
            precision=lax.Precision.HIGHEST,
            preferred_element_type=F32,
        )
        skip_ref[...] = lax.dot_general(
            pick((channels, side), 1).astype(F32),
            half,
            (((1,), (0,)), ((), ())),
            precision=lax.Precision.HIGHEST,
            preferred_element_type=F32,
        )


def mix(inputs, cot, weight, planes, after=()):
    channels, rows, _ = inputs.shape
    count = 16
    side = channels * PLANES
    spec = pl.BlockSpec((channels, count * planes, NZ), lambda x: (0, x, 0))
    return pl.pallas_call(
        functools.partial(mix_body, planes=planes, count=count),
        out_shape=(
            jax.ShapeDtypeStruct(inputs.shape, BF16),
            jax.ShapeDtypeStruct((channels, LANES), F32),
        ),
        grid=(NX // count,),
        in_specs=[spec, spec, whole((channels, channels))] + [ANYWHERE] * len(after),
        out_specs=(spec, whole((channels, LANES))),
        scratch_shapes=[pltpu.VMEM((side, side), F32), pltpu.VMEM((side, side), BF16)],
        compiler_params=params(),
        cost_estimate=cost(22),
        name="mix",
    )(inputs, cot, weight, *after)


def x_then_z(
    received, mixed_ref, table_x, table_z, out_ref, real_ref, imag_ref, planes
):
    part = 2 * MX // len(received)
    for y in range(0, planes, 2):
        pair = [
            jnp.concatenate(
                [
                    ref[side, at * part : (at + 1) * part, :]
                    for side in range(2)
                    for ref in received
                ],
                axis=0,
            ).astype(BF16)
            for at in (y, y + 1)
        ]
        found = dot(table_x[0], jnp.concatenate(pair, axis=1))
        for place in range(2):
            lane = slice(place * LANES, (place + 1) * LANES)
            real_ref[pl.ds(y + place, NX, stride=planes), :] = found[:NX, lane]
            imag_ref[pl.ds(y + place, NX, stride=planes), :] = found[NX:, lane]
    rows = NX * planes
    step = min(rows, 256)
    for start in range(0, rows, step):
        place = slice(start, start + step)
        line = jnp.concatenate([real_ref[place, :], imag_ref[place, :]], axis=1).astype(BF16)
        found = dot(line, table_z[...])
        for c in range(GROUP):
            mixed = mixed_ref[c, place, :].astype(F32)
            out_ref[c, place, :] = (found[:, c * NZ : (c + 1) * NZ] + mixed).astype(BF16)


def grid_body(relay_ref, *refs, planes, relays, root):
    received, refs = refs[:relays], refs[relays:]
    if root is None:
        mixed_ref, table_x, table_z = refs[:3]
        out_ref, real_ref, imag_ref = refs[-3:]
    else:
        skips, refs = refs[:relays], refs[relays:]
        mixed_ref, table_x, table_z = refs[:3]
        out_ref, total_ref, real_ref, imag_ref = refs[-4:]

        @pl.when(pl.program_id(0) == 0)
        def _():
            total = sum(ref[0] for ref in skips)
            total_ref[...] = total[:, : total_ref.shape[1]] / root

    x_then_z(received, mixed_ref, table_x, table_z, out_ref, real_ref, imag_ref, planes)


def grid_of(relay, received, mixed, first, groups, planes, root=None, after=()):
    relays = len(received)
    channels = mixed.shape[0]
    per_group = planes * 2 * MX // relays
    spec = pl.BlockSpec((GROUP, NX * planes, NZ), lambda g, at: (g + first, 0, 0))
    in_specs = [pl.BlockSpec((2, per_group, LANES), lambda g, at: (0, g, 0))] * relays
    operands = list(received)
    out_shape = (jax.ShapeDtypeStruct(mixed.shape, BF16),)
    out_specs = (spec,)
    if root is not None:
        extra = groups * per_group // channels
        in_specs += [pl.BlockSpec((1, channels, LANES), lambda g, at: (0, extra, 0))] * relays
        operands += received
        out_shape += (jax.ShapeDtypeStruct((channels, channels), F32),)
        out_specs += (fixed((channels, channels)),)
    in_specs += [
        spec,
        pl.BlockSpec((1, 2 * NX, 4 * MX), lambda g, at: (at[0], 0, 0)),
        fixed((2 * LANES, GROUP * NZ)),
    ] + [ANYWHERE] * len(after)
    operands += [mixed, x_inverse_table(relays), z_inverse_table(), *after]
    return pl.pallas_call(
        functools.partial(grid_body, planes=planes, relays=relays, root=root),
        out_shape=out_shape,
        grid_spec=pltpu.PrefetchScalarGridSpec(
            num_scalar_prefetch=1,
            grid=(groups,),
            in_specs=in_specs,
            out_specs=out_specs,
            scratch_shapes=[
                pltpu.VMEM((NX * planes, LANES), F32),
                pltpu.VMEM((NX * planes, LANES), F32),
            ],
        ),
        input_output_aliases={1 + (relays if root is None else 2 * relays): 0},
        compiler_params=params(),
        cost_estimate=cost(9),
        name="to_grid",
    )(relay, *operands)


def cross_body(*refs, samples):
    lefts, rights, out_ref = refs[:samples], refs[samples : 2 * samples], refs[-1]
    channels, own, lanes = out_ref.shape[1:]
    kz = lax.broadcasted_iota(jnp.int32, (own, lanes), 1) // (2 * MY) % MZ
    scale = jnp.where(kz == 0, 1.0, 2.0) / float(NX * NY * NZ)
    scaled = [(ref[:own, :] * scale, ref[own : 2 * own, :] * scale) for ref in rights]
    for i in range(channels):
        real = imag = None
        for b in range(samples):
            left_real = lefts[b][i : i + 1, :]
            left_imag = lefts[b][channels + i : channels + i + 1, :]
            right_real, right_imag = scaled[b]
            one = left_real * right_real + left_imag * right_imag
            two = left_real * right_imag - left_imag * right_real
            real = one if real is None else real + one
            imag = two if imag is None else imag + two
        out_ref[0, i] = real
        out_ref[1, i] = imag


def cross(lefts, rights, after=()):
    rows, modes = lefts[0].shape
    channels = rows // 2
    own = (rights[0].shape[0] - SUBLANES) // 2
    lanes = 2 * MY * MZ
    return pl.pallas_call(
        functools.partial(cross_body, samples=len(lefts)),
        out_shape=jax.ShapeDtypeStruct((2, channels, own, modes), F32),
        grid=(modes // lanes,),
        in_specs=[pl.BlockSpec((rows, lanes), lambda k: (0, k))] * len(lefts)
        + [pl.BlockSpec((2 * own + SUBLANES, lanes), lambda k: (0, k))] * len(rights)
        + [ANYWHERE] * len(after),
        out_specs=pl.BlockSpec((2, channels, own, lanes), lambda k: (0, 0, 0, k)),
        compiler_params=params(),
        cost_estimate=cost(6),
        name="cross",
    )(*lefts, *rights, *after)


def exchange_near(values):
    spaces = lax.axis_size("space")
    groups = [list(range(spaces // 2)), list(range(spaces // 2, spaces))]
    return lax.all_to_all(
        values, "space", split_axis=0, concat_axis=0, axis_index_groups=groups, tiled=True
    )


def spread(blocks, axis):
    size = lax.axis_size(axis)
    return [blocks[0]] + [
        lax.ppermute(blocks[d], axis, [(s, s ^ d) for s in range(size)])
        for d in range(1, len(blocks))
    ]


def exchange_far(values, turned=False):
    spaces = lax.axis_size("space")
    pairs = [(s, (s + spaces // 2) % spaces) for s in range(spaces)]
    pairs = pairs[::-1] if turned else pairs
    return lax.ppermute(values, "space", pairs)


HIGHEST = lax.Precision.HIGHEST


def phase_table(length, count, signed):
    points = jnp.arange(length, dtype=jnp.int32)
    orders = jnp.arange(count, dtype=jnp.int32)
    if signed:
        orders = jnp.where(orders < count // 2, orders, orders - count)
    residues = jnp.mod(points[:, None] * orders[None, :], length)
    radians = residues.astype(jnp.float32) * (2.0 * math.pi / length)
    return (jnp.cos(radians), jnp.sin(radians))


def forward_block(cosine, sine):
    return jnp.stack(
        [jnp.stack([cosine, -sine], axis=1), jnp.stack([sine, cosine], axis=1)], axis=0
    )


def inverse_block(cosine, sine):
    cos_rows = cosine.T
    sin_rows = sine.T
    return jnp.stack(
        [jnp.stack([cos_rows, sin_rows], axis=1), jnp.stack([-sin_rows, cos_rows], axis=1)], axis=0
    )


def local_spectrum(grid_in):
    cos_x, sin_x = phase_table(NX, 2 * MX, True)
    table_x = jnp.stack([cos_x, -sin_x], axis=1).astype(jnp.bfloat16)
    section_x = jnp.einsum(
        "scxyz,xpa->scpayz", grid_in, table_x, preferred_element_type=jnp.float32
    )
    cos_z, sin_z = phase_table(NZ, MZ, False)
    section_z = jnp.einsum(
        "scpayz,pzqk->scqyak", section_x, forward_block(cos_z, sin_z), precision=HIGHEST
    )
    return section_z.reshape(
        section_z.shape[0], section_z.shape[1], 2, section_z.shape[3], 2 * MX * MZ
    )


def along_y(spectra):
    cos_y, sin_y = phase_table(NY, 2 * MY, True)
    section_y = jnp.einsum(
        "scpym,pyqk->scqmk", spectra, forward_block(cos_y, sin_y), precision=HIGHEST
    )
    return section_y.reshape(section_y.shape[0], section_y.shape[1], 2, section_y.shape[3] * 2 * MY)


def both_along_y(spectra_pair):
    return (along_y(spectra_pair[0]), along_y(spectra_pair[1]))


def to_grid(spectra):
    shaped = spectra.reshape(spectra.shape[0], spectra.shape[1], 2, spectra.shape[3], 2 * MX, MZ)
    cos_z, sin_z = phase_table(NZ, MZ, False)
    grid_z = jnp.einsum(
        "scpyak,pkqz->scqayz", shaped, inverse_block(cos_z, sin_z), precision=HIGHEST
    )
    cos_x, sin_x = phase_table(NX, 2 * MX, True)
    table_x = jnp.stack([cos_x.T, -sin_x.T], axis=0)
    return jnp.einsum("scpayz,pax->scxyz", grid_z, table_x, precision=HIGHEST)


def cross_terms(spec_left, spec_right):
    real_part = jnp.einsum(
        "sim,som->iom", spec_left[:, :, 0], spec_right[:, :, 0], precision=HIGHEST
    )
    real_part = real_part + jnp.einsum(
        "sim,som->iom", spec_left[:, :, 1], spec_right[:, :, 1], precision=HIGHEST
    )
    imag_part = jnp.einsum(
        "sim,som->iom", spec_left[:, :, 0], spec_right[:, :, 1], precision=HIGHEST
    )
    imag_part = imag_part - jnp.einsum(
        "sim,som->iom", spec_left[:, :, 1], spec_right[:, :, 0], precision=HIGHEST
    )
    return jnp.stack([real_part, imag_part], axis=0)


def contract(weight_part, spec_part):
    return jnp.einsum("iom,som->sim", weight_part, spec_part, preferred_element_type=jnp.float32)


def skip_gradient(grid_in, cot_pre):
    partial_sum = jnp.einsum(
        "sixyz,soxyz->io", grid_in, cot_pre, preferred_element_type=jnp.float32
    )
    summed = lax.psum(partial_sum, ("batch", "space"))
    return summed / math.sqrt(grid_in.shape[0] * lax.axis_size("batch") * NX * NY * NZ)


def general(inputs, pre_act, cotangent, spectral_weight, skip_weight):
    samples = inputs.shape[0]
    channels = inputs.shape[1]
    slope_pre = slope(pre_act.astype(jnp.float32))
    cot_pre = (cotangent.astype(jnp.float32) * slope_pre).astype(jnp.bfloat16)
    spec_u, spec_e = both_along_y(
        (
            lax.all_to_all(
                local_spectrum(inputs), "space", split_axis=4, concat_axis=3, tiled=True
            ),
            lax.all_to_all(
                local_spectrum(cot_pre), "space", split_axis=4, concat_axis=3, tiled=True
            ),
        )
    )
    mode_count = spec_u.shape[3]
    position = jnp.arange(mode_count, dtype=jnp.int32)
    kxz_index = lax.axis_index("space") * (mode_count // (2 * MY)) + position // (2 * MY)
    mode_weights = jnp.where(kxz_index % MZ == 0, 1.0, 2.0).astype(jnp.float32) / float(
        NX * NY * NZ
    )
    mode_grad = lax.psum_scatter(
        cross_terms(spec_u, spec_e), "batch", scatter_dimension=2, tiled=True
    )
    grad_spectral = mode_grad * mode_weights
    rounded = spec_e.astype(jnp.bfloat16)
    weight_real = spectral_weight[0]
    weight_imag = spectral_weight[1]
    back_real = contract(weight_real, rounded[:, :, 0]) + contract(weight_imag, rounded[:, :, 1])
    back_imag = contract(weight_real, rounded[:, :, 1]) - contract(weight_imag, rounded[:, :, 0])
    back_modes = jnp.stack([back_real, back_imag], axis=2) * mode_weights
    shaped = back_modes.reshape(samples, channels, 2, mode_count // (2 * MY), 2 * MY)
    cos_y, sin_y = phase_table(NY, 2 * MY, True)
    grid_y = jnp.einsum("scpmk,pkqy->scqym", shaped, inverse_block(cos_y, sin_y), precision=HIGHEST)
    spatial = to_grid(lax.all_to_all(grid_y, "space", split_axis=3, concat_axis=4, tiled=True))
    mixed = jnp.einsum("io,soxyz->sixyz", skip_weight, cot_pre, preferred_element_type=jnp.float32)
    grad_inputs = (spatial + mixed).astype(jnp.bfloat16)
    grad_skip = skip_gradient(inputs, cot_pre)
    return (grad_inputs, grad_spectral, grad_skip)


def on_device(inputs, pre_act, cotangent, spectral_weight, skip_weight):
    samples, channels, _, planes, _ = inputs.shape
    spaces = lax.axis_size("space")
    batches = lax.axis_size("batch")
    if samples != 1 or spaces < 2 or spaces & (spaces - 1) or (2 * MX) % spaces or planes % 16 or channels % (4 * GROUP):
        return general(inputs, pre_act, cotangent, spectral_weight, skip_weight)
    if batches & (batches - 1) or channels % (SUBLANES * batches):
        return general(inputs, pre_act, cotangent, spectral_weight, skip_weight)
    kx_local = 2 * MX // spaces
    flat = (channels, NX * planes, NZ)
    groups = channels // GROUP
    inputs, pre_act, cotangent = (v.reshape(flat) for v in (inputs, pre_act, cotangent))
    half = (lax.axis_index("space") // (spaces // 2)).astype(jnp.int32).reshape(1)
    relay = (lax.axis_index("space") % (spaces // 2)).astype(jnp.int32).reshape(1)
    batch = lax.axis_index("batch").astype(jnp.int32).reshape(1)
    middle = groups // 2
    (send_u,) = forward((inputs,), 0, groups, planes, spaces, False)
    near_u = exchange_near(send_u)
    send_e, cot_pre = forward(
        (pre_act, cotangent), 0, groups, planes, spaces, True, after=(send_u,)
    )
    near_e = exchange_near(send_e)
    part_u = partial_sums(half, near_u, groups, kx_local, "partial_u", after=(send_e,))
    far_u = exchange_far(part_u)
    mixed, skip_part = mix(inputs, cot_pre, skip_weight, planes, after=(part_u,))
    part_e = partial_sums(half, near_e, groups, kx_local, "partial_e", riding=(skip_part,))
    far_e = exchange_far(part_e)
    hat_u = finish_u(half, near_u, far_u, channels, kx_local, after=(part_e,))
    all_u = spread([hat_u] * batches, "batch")
    own_e, rounded, modes_a = finish_e(
        batch, half, near_e, far_e, spectral_weight, skip_part, kx_local, batches, tuple(all_u[1:])
    )
    far_a = exchange_far(modes_a)
    all_e = spread(own_e, "batch")
    modes_b = finish_rest(rounded, spectral_weight, kx_local)
    modes_b, far_a = lax.optimization_barrier((modes_b, far_a))
    far_b = exchange_far(modes_b, turned=True)
    send_a = expand(half, relay, modes_a, far_a, spaces // 2, middle, kx_local)
    near_a = spread(send_a, "space")
    grad_spectral = cross(all_u, all_e, after=send_a[:1])
    send_b = expand(
        half,
        relay,
        modes_b,
        far_b,
        spaces // 2,
        middle,
        kx_local,
        all_e,
        channels,
        (grad_spectral,),
    )
    near_b = spread(send_b, "space")
    (grad_inputs,) = grid_of(relay, near_a, mixed, 0, middle, planes, after=send_b[:1])
    root = math.sqrt(samples * batches * NX * NY * NZ)
    grad_inputs, grad_skip = grid_of(relay, near_b, grad_inputs, middle, middle, planes, root)
    return (
        grad_inputs.reshape(samples, channels, NX, planes, NZ),
        grad_spectral,
        grad_skip,
    )


def solution(mesh):
    placed = (
        P("batch", None, None, "space", None),
        P("batch", None, None, "space", None),
        P("batch", None, None, "space", None),
        P(None, None, None, "space"),
        P(),
    )
    return jax.shard_map(
        on_device,
        mesh=mesh,
        in_specs=placed,
        out_specs=(P("batch", None, None, "space", None), P(None, None, "batch", "space"), P()),
        check_vma=False,
    )
```

```python
import functools
import math

import jax
import jax.numpy as jnp
import ml_dtypes
import numpy as np
from jax import lax
from jax.experimental import pallas as pl
from jax.experimental.pallas import tpu as pltpu
from jax.sharding import PartitionSpec as P

NX = 128
NY = 128
NZ = 128
MX = 16
MY = 16
MZ = 16
GROUP = 8
LANES = GROUP * MZ
BF16 = jnp.bfloat16
F32 = jnp.float32
VMEM_LIMIT = 62 * 1024 * 1024


def cost(microseconds):
    return pl.CostEstimate(flops=int(microseconds * 2e9), bytes_accessed=1, transcendentals=0)


def waves(length, count, signed):
    points = np.arange(length)
    orders = np.arange(count)
    if signed:
        orders = np.where(orders < count // 2, orders, orders - count)
    radians = np.mod(points[:, None] * orders[None, :], length) * (2.0 * math.pi / length)
    return np.cos(radians), np.sin(radians)


def rounded_table(table):
    return np.asarray(table, np.float32).astype(ml_dtypes.bfloat16)


def z_forward_table():
    cos, sin = waves(NZ, MZ, False)
    table = np.zeros((GROUP, NZ, 2, GROUP, MZ))
    for c in range(GROUP):
        table[c, :, 0, c, :] = cos
        table[c, :, 1, c, :] = -sin
    return jnp.asarray(rounded_table(table.reshape(GROUP * NZ, 2 * LANES)))


def z_inverse_table():
    cos, sin = waves(NZ, MZ, False)
    table = np.zeros((2, GROUP, MZ, GROUP, NZ))
    for c in range(GROUP):
        table[0, c, :, c, :] = cos.T
        table[1, c, :, c, :] = -sin.T
    return jnp.asarray(rounded_table(table.reshape(2 * LANES, GROUP * NZ)))


def x_forward_table(spaces):
    cos, sin = waves(NX, 2 * MX, True)
    cos = cos.T.reshape(spaces, 2 * MX // spaces, NX)
    sin = sin.T.reshape(spaces, 2 * MX // spaces, NX)
    table = np.stack([np.stack([cos, sin], axis=2), np.stack([-sin, cos], axis=2)], axis=1)
    return jnp.asarray(rounded_table(table.reshape(4 * MX, 2 * NX)))


def x_inverse_table(relays):
    cos, sin = waves(NX, 2 * MX, True)
    cos = cos.reshape(NX, 2, relays, MX // relays)
    sin = sin.reshape(NX, 2, relays, MX // relays)
    table = np.stack([np.stack([cos, -sin], axis=3), np.stack([sin, cos], axis=3)], axis=0)
    place = np.arange(relays)
    table = np.stack([table[:, :, :, place ^ r] for r in range(relays)])
    return jnp.asarray(rounded_table(table.reshape(relays, 2 * NX, 4 * MX)))


def split_table(table):
    high = rounded_table(table)
    low = rounded_table(table - high.astype(np.float64))
    return jnp.asarray(np.concatenate([high, high, low], axis=-1))


def y_forward_table(kx_local):
    cos, sin = waves(NY, 2 * MY, True)
    table = np.zeros((2, kx_local, 2 * MY, NY, 2, kx_local))
    for j in range(kx_local):
        table[0, j, :, :, 0, j] = cos.T
        table[0, j, :, :, 1, j] = sin.T
        table[1, j, :, :, 0, j] = -sin.T
        table[1, j, :, :, 1, j] = cos.T
    table = table.reshape(4 * MY * kx_local, 2, NY * kx_local)
    return split_table(table.swapaxes(0, 1))


def y_inverse_table(kx_local):
    cos, sin = waves(NY, 2 * MY, True)
    table = np.zeros((NY, 2, kx_local, 2, kx_local, 2 * MY))
    for j in range(kx_local):
        table[:, 0, j, 0, j, :] = cos
        table[:, 0, j, 1, j, :] = -sin
        table[:, 1, j, 0, j, :] = sin
        table[:, 1, j, 1, j, :] = cos
    return split_table(table.reshape(2, NY * kx_local, 4 * MY * kx_local))


def dot(left, right):
    return lax.dot_general(left, right, (((1,), (0,)), ((), ())), preferred_element_type=F32)


def dot_split(table, values):
    high = values.astype(BF16)
    low = (values - high.astype(F32)).astype(BF16)
    return dot(table, jnp.concatenate([high, low, high], axis=0))


def params(count=1):
    return pltpu.CompilerParams(
        vmem_limit_bytes=VMEM_LIMIT, dimension_semantics=("arbitrary",) * count
    )


def z_then_x(load, table_z, table_x, send_ref, real_ref, imag_ref, planes, spaces, blocks):
    rows = NX * planes // blocks
    block = pl.program_id(1)
    step = min(rows, 512)
    for start in range(0, rows, step):
        line = jnp.concatenate([load(c, start, step) for c in range(GROUP)], axis=1)
        found = dot(line, table_z[...])
        place = pl.ds(pl.multiple_of(block * rows + start, step), step)
        real_ref[place, :] = found[:, :LANES]
        imag_ref[place, :] = found[:, LANES:]
    part = 4 * MX // spaces

    @pl.when(block == blocks - 1)
    def _():
        for y in range(0, planes, 2):
            pair = []
            for at in (y, y + 1):
                real = real_ref[pl.ds(at, NX, stride=planes), :]
                imag = imag_ref[pl.ds(at, NX, stride=planes), :]
                pair.append(jnp.concatenate([real, imag], axis=0).astype(BF16))
            found = dot(table_x[...], jnp.concatenate(pair, axis=1))
            for place in range(2):
                for s in range(spaces):
                    relay, side = s % (spaces // 2), s // (spaces // 2)
                    rows_of = slice((y + place) * part, (y + place + 1) * part)
                    send_ref[relay, side, rows_of, :] = found[
                        s * part : (s + 1) * part, place * LANES : (place + 1) * LANES
                    ]


def forward_plain(
    field_ref, table_z, table_x, *refs, planes, spaces, blocks
):
    send_ref, real_ref, imag_ref = refs[-3:]

    def load(c, start, step):
        return field_ref[c, start : start + step, :]

    z_then_x(load, table_z, table_x, send_ref, real_ref, imag_ref, planes, spaces, blocks)


def slope(values):
    normal_cdf = 0.5 * (1.0 + lax.erf(values * (1.0 / math.sqrt(2.0))))
    density = jnp.exp(-0.5 * values * values) * (1.0 / math.sqrt(2.0 * math.pi))
    return normal_cdf + values * density


def forward_cot(pre_ref, cot_ref, table_z, table_x, *refs, planes, spaces, blocks):
    send_ref, out_ref, real_ref, imag_ref = refs[-4:]

    def load(c, start, step):
        pre = pre_ref[c, start : start + step, :].astype(F32)
        cot = cot_ref[c, start : start + step, :].astype(F32)
        made = (cot * slope(pre)).astype(BF16)
        out_ref[c, start : start + step, :] = made
        return made

    z_then_x(load, table_z, table_x, send_ref, real_ref, imag_ref, planes, spaces, blocks)


def whole(shape):
    return pl.BlockSpec(shape, lambda *_: (0,) * len(shape))


ANYWHERE = pl.BlockSpec(memory_space=pl.ANY)


def forward(fields, first, groups, planes, spaces, cot, after=()):
    channels, rows, _ = fields[0].shape
    blocks = 1
    part = 4 * MX // spaces
    field_spec = pl.BlockSpec((GROUP, rows // blocks, NZ), lambda g, r: (g + first, r, 0))
    send_shape = jax.ShapeDtypeStruct((spaces // 2, 2, groups * planes * part, LANES), F32)
    send_spec = pl.BlockSpec((spaces // 2, 2, planes * part, LANES), lambda g, r: (0, 0, g, 0))
    out_shape, out_specs = (send_shape,), (send_spec,)
    if cot:
        out_shape += (jax.ShapeDtypeStruct(fields[0].shape, BF16),)
        out_specs += (field_spec,)
    body = forward_cot if cot else forward_plain
    return pl.pallas_call(
        functools.partial(body, planes=planes, spaces=spaces, blocks=blocks),
        out_shape=out_shape,
        grid=(groups, blocks),
        in_specs=[field_spec] * len(fields)
        + [whole((GROUP * NZ, 2 * LANES)), whole((4 * MX, 2 * NX))]
        + [ANYWHERE] * len(after),
        out_specs=out_specs,
        scratch_shapes=[pltpu.VMEM((rows, LANES), F32), pltpu.VMEM((rows, LANES), F32)],
        compiler_params=params(2),
        cost_estimate=cost(25 if cot else 11),
        name="forward_e" if cot else "forward_u",
    )(*fields, z_forward_table(), x_forward_table(spaces), *after)


def half_sums(near_ref, table, g, count):
    relays = near_ref.shape[0]
    per_group = table.shape[2] // 3 // relays
    data = jnp.concatenate(
        [
            jnp.concatenate(
                [
                    near_ref[r, 0, at * per_group : (at + 1) * per_group, :]
                    for at in range(g, g + count)
                ],
                axis=1,
            )
            for r in range(relays)
        ],
        axis=0,
    )
    return dot_split(table[0], data)


def partial_body(half_ref, near_ref, table, *refs, groups, riding):
    out_ref = refs[-1]
    rows = table.shape[1]
    for g in range(0, groups, 2):
        found = half_sums(near_ref, table, g, 2)
        out_ref[g * rows : (g + 1) * rows, :] = found[:, :LANES]
        out_ref[(g + 1) * rows : (g + 2) * rows, :] = found[:, LANES:]
    if riding:
        out_ref[groups * rows :, :] = refs[0][...]


def table_spec(table, side):
    return pl.BlockSpec((1,) + table.shape[1:], lambda *at: (side(at[-1][0]), 0, 0))


def near_spec(near, side):
    shape = (near.shape[0], 1) + near.shape[2:]
    return pl.BlockSpec(shape, lambda *at: (0, side(at[-1][0]), 0, 0))


def own_side(half):
    return half


def other_side(half):
    return 1 - half


def fixed(shape):
    return pl.BlockSpec(shape, lambda *at: (0,) * len(shape))


def partial_sums(half, near, groups, kx_local, name, riding=(), after=()):
    table = y_forward_table(kx_local)
    rows = groups * table.shape[1] + sum(v.shape[0] for v in riding)
    return pl.pallas_call(
        functools.partial(partial_body, groups=groups, riding=bool(riding)),
        out_shape=jax.ShapeDtypeStruct((rows, LANES), F32),
        grid_spec=pltpu.PrefetchScalarGridSpec(
            num_scalar_prefetch=1,
            grid=(1,),
            in_specs=[near_spec(near, other_side), table_spec(table, own_side)]
            + [fixed(v.shape) for v in riding]
            + [ANYWHERE] * len(after),
            out_specs=fixed((rows, LANES)),
        ),
        compiler_params=params(),
        cost_estimate=cost(3),
        name=name,
    )(half, near, table, *riding, *after)


def unfold_y(near_ref, far_ref, table, lines, store, kx_local):
    width = kx_local * 2 * MY
    channels = lines.shape[1] // MZ
    groups = channels // GROUP
    for g in range(0, groups, 2):
        pair = half_sums(near_ref, table, g, 2)
        for at in (g, g + 1):
            found = pair[:, (at - g) * LANES : (at - g + 1) * LANES] + far_ref[
                2 * at * width : 2 * (at + 1) * width, :
            ]
            for part in range(2):
                lines[part, at * LANES : (at + 1) * LANES, :] = found[
                    part * width : (part + 1) * width, :
                ].T
    for part in range(2):
        for kz in range(MZ):
            piece = lines[part, pl.ds(kz, channels, stride=MZ), :]
            for j in range(kx_local):
                store(
                    part,
                    (j * MZ + kz) * 2 * MY,
                    piece[:, j * 2 * MY : (j + 1) * 2 * MY],
                )


def fold_modes(back, lines, send_ref, kx_local):
    channels = back.shape[1]
    for part in range(2):
        for kz in range(MZ):
            pieces = [
                back[part, :, (j * MZ + kz) * 2 * MY : (j * MZ + kz + 1) * 2 * MY]
                for j in range(kx_local)
            ]
            lines[part, pl.ds(kz, channels, stride=MZ), :] = jnp.concatenate(pieces, axis=1)
    width = kx_local * 2 * MY
    for g in range(channels // GROUP):
        for part in range(2):
            row = (2 * g + part) * width
            send_ref[row : row + width, :] = lines[part, g * LANES : (g + 1) * LANES, :].T


SUBLANES = 8


def spectrum_u(half_ref, near_ref, far_ref, table, *refs, kx_local):
    hat_ref, lines = refs[-2:]
    channels = hat_ref.shape[0] // 2

    def store(part, column, values):
        hat_ref[part * channels : (part + 1) * channels, column : column + 2 * MY] = values

    unfold_y(near_ref, far_ref, table, lines, store, kx_local)


def finish_u(half, near, far, channels, kx_local, after=()):
    table = y_forward_table(kx_local)
    shape = (2 * channels, kx_local * MZ * 2 * MY)
    return pl.pallas_call(
        functools.partial(spectrum_u, kx_local=kx_local),
        out_shape=jax.ShapeDtypeStruct(shape, F32),
        grid_spec=pltpu.PrefetchScalarGridSpec(
            num_scalar_prefetch=1,
            grid=(1,),
            in_specs=[near_spec(near, own_side), fixed(far.shape), table_spec(table, own_side)]
            + [ANYWHERE] * len(after),
            out_specs=fixed(shape),
            scratch_shapes=[pltpu.VMEM((2, channels * MZ, kx_local * 2 * MY), F32)],
        ),
        compiler_params=params(),
        cost_estimate=cost(4),
        name="finish_u",
    )(half, near, far, table, *after)


def mode_scale(kz):
    return (1.0 if kz == 0 else 2.0) / float(NX * NY * NZ)


def through_weight(weight_ref, rounded, back, per_step, modes):
    step = pl.program_id(0)
    for start in range(0, modes, 128):
        lane = slice(start, start + 128)
        real = rounded[0, :, lane]
        imag = rounded[1, :, lane]
        reals, imags = [], []
        for i in range(per_step):
            weight_real = weight_ref[0, i, :, lane].astype(F32)
            weight_imag = weight_ref[1, i, :, lane].astype(F32)
            reals.append(
                jnp.sum(weight_real * real + weight_imag * imag, axis=0, keepdims=True)
            )
            imags.append(
                jnp.sum(weight_real * imag - weight_imag * real, axis=0, keepdims=True)
            )
        rows = pl.ds(pl.multiple_of(step * per_step, per_step), per_step)
        back[0, rows, lane] = jnp.concatenate(reals, axis=0)
        back[1, rows, lane] = jnp.concatenate(imags, axis=0)


def spectrum_e(
    batch_ref,
    half_ref,
    near_ref,
    far_ref,
    weight_ref,
    table,
    skip_ref,
    *refs,
    kx_local,
    per_step,
    batches,
):
    rounded, send_ref, hat, lines, back = refs[-5:]
    own_refs = refs[-5 - batches : -5]
    channels = skip_ref.shape[0]
    own = channels // batches

    @pl.when(pl.program_id(0) == 0)
    def _():
        def store(part, column, values):
            hat[part, :, column : column + 2 * MY] = values
            rounded[part, :, column : column + 2 * MY] = values.astype(BF16).astype(
                F32
            ) * mode_scale((column // (2 * MY)) % MZ)

        unfold_y(near_ref, far_ref, table, lines, store, kx_local)
        skip = skip_ref[...] + far_ref[far_ref.shape[0] - channels :, :]
        for d in range(batches):
            first = jnp.bitwise_xor(batch_ref[0], d) * own
            rows = pl.ds(pl.multiple_of(first, own), own)
            own_refs[d][:own, :] = hat[0, rows, :]
            own_refs[d][own : 2 * own, :] = hat[1, rows, :]
            own_refs[d][2 * own :, :] = jnp.zeros((SUBLANES, hat.shape[2]), F32)
            for k in range(channels // SUBLANES):
                own_refs[d][2 * own :, k * LANES : (k + 1) * LANES] = skip[
                    k * SUBLANES : (k + 1) * SUBLANES, :
                ]

    through_weight(weight_ref, rounded, back, per_step, kx_local * MZ * 2 * MY)

    @pl.when(pl.program_id(0) == pl.num_programs(0) - 1)
    def _():
        fold_modes(back, lines, send_ref, kx_local)


def spectrum_rest(rounded, weight_ref, *refs, kx_local, per_step):
    send_ref, lines, back = refs[-3:]
    through_weight(weight_ref, rounded, back, per_step, kx_local * MZ * 2 * MY)

    @pl.when(pl.program_id(0) == pl.num_programs(0) - 1)
    def _():
        fold_modes(back, lines, send_ref, kx_local)


def finish_e(batch, half, near, far, weight, skip, kx_local, batches, after=()):
    channels = skip.shape[0]
    modes = kx_local * MZ * 2 * MY
    per_step = 8
    near_half = channels // 2
    table = y_forward_table(kx_local)
    own = jax.ShapeDtypeStruct((2 * channels // batches + SUBLANES, modes), F32)
    spectrum = jax.ShapeDtypeStruct((2, channels, modes), F32)
    send = jax.ShapeDtypeStruct((near_half // GROUP * 2 * kx_local * 2 * MY, LANES), F32)
    *owns, rounded, sent = pl.pallas_call(
        functools.partial(spectrum_e, kx_local=kx_local, per_step=per_step, batches=batches),
        out_shape=(own,) * batches + (spectrum, send),
        grid_spec=pltpu.PrefetchScalarGridSpec(
            num_scalar_prefetch=2,
            grid=(near_half // per_step,),
            in_specs=[
                near_spec(near, own_side),
                fixed(far.shape),
                pl.BlockSpec((2, per_step, channels, modes), lambda i, *at: (0, i, 0, 0)),
                table_spec(table, own_side),
                fixed(skip.shape),
            ]
            + [ANYWHERE] * len(after),
            out_specs=(fixed(own.shape),) * batches + (fixed(spectrum.shape), fixed(send.shape)),
            scratch_shapes=[
                pltpu.VMEM((2, channels, modes), F32),
                pltpu.VMEM((2, channels * MZ, kx_local * 2 * MY), F32),
                pltpu.VMEM((2, near_half, modes), F32),
            ],
        ),
        compiler_params=params(),
        cost_estimate=cost(8),
        name="finish_e",
    )(batch, half, near, far, weight, table, skip, *after)
    return owns, rounded, sent


def finish_rest(rounded, weight, kx_local, after=()):
    _, channels, modes = rounded.shape
    per_step = 8
    rest = channels // 2
    steps = rest // per_step
    send = jax.ShapeDtypeStruct((rest // GROUP * 2 * kx_local * 2 * MY, LANES), F32)
    return pl.pallas_call(
        functools.partial(spectrum_rest, kx_local=kx_local, per_step=per_step),
        out_shape=send,
        grid=(steps,),
        in_specs=[
            whole(rounded.shape),
            pl.BlockSpec((2, per_step, channels, modes), lambda i: (0, i + steps, 0, 0)),
        ]
        + [ANYWHERE] * len(after),
        out_specs=whole(send.shape),
        scratch_shapes=[
            pltpu.VMEM((2, rest * MZ, kx_local * 2 * MY), F32),
            pltpu.VMEM((2, rest, modes), F32),
        ],
        compiler_params=params(),
        cost_estimate=cost(5),
        name="finish_rest",
    )(rounded, weight, *after)


def expand_body(
    half_ref, relay_ref, own_ref, far_ref, table, *refs, groups, channels, relays, riding
):
    send_refs = refs[-relays - 1 : -1]
    lines = refs[-1]
    per_group = table.shape[1] // relays
    modes = table.shape[2] // 3
    half = half_ref[0]
    at_line = 0
    for ref, side in ((own_ref, half), (far_ref, 1 - half)):
        for g in range(0, groups, 2):
            data = jnp.concatenate(
                [ref[at * modes : (at + 1) * modes, :] for at in (g, g + 1)], axis=1
            )
            lines[at_line] = dot_split(table[0], data)
            for d in range(relays):
                place = jnp.bitwise_xor(relay_ref[0], d) * per_group
                rows = pl.ds(pl.multiple_of(place, per_group), per_group)
                for at in (g, g + 1):
                    send_refs[d][side, at * per_group : (at + 1) * per_group, :] = lines[
                        at_line, rows, (at - g) * LANES : (at - g + 1) * LANES
                    ]
            at_line += 1
    if channels:
        skip = sum(ref[...] for ref in refs[:riding])
        for d in range(relays):
            for side in range(2):
                for k in range(channels // SUBLANES):
                    row = groups * per_group + k * SUBLANES
                    send_refs[d][side, row : row + SUBLANES, :] = skip[
                        :, k * LANES : (k + 1) * LANES
                    ]


def expand(half, relay, own, far, relays, groups, kx_local, riding=(), channels=0, after=()):
    table = y_inverse_table(kx_local)
    shape = (2, groups * table.shape[1] // relays + channels, LANES)
    skip_specs = [
        pl.BlockSpec(
            (SUBLANES, channels // SUBLANES * LANES),
            lambda *at: (riding[0].shape[0] // SUBLANES - 1, 0),
        )
        for _ in riding
    ]
    return pl.pallas_call(
        functools.partial(
            expand_body, groups=groups, channels=channels, relays=relays, riding=len(riding)
        ),
        out_shape=(jax.ShapeDtypeStruct(shape, F32),) * relays,
        grid_spec=pltpu.PrefetchScalarGridSpec(
            num_scalar_prefetch=2,
            grid=(1,),
            in_specs=[
                fixed(own.shape),
                fixed(far.shape),
                pl.BlockSpec((1,) + table.shape[1:], lambda i, half, relay: (half[0], 0, 0)),
            ]
            + skip_specs
            + [ANYWHERE] * len(after),
            out_specs=(fixed(shape),) * relays,
            scratch_shapes=[pltpu.VMEM((groups, table.shape[1], 2 * LANES), F32)],
        ),
        compiler_params=params(),
        cost_estimate=cost(60),
        name="expand",
    )(half, relay, own, far, table, *riding, *after)


PLANES = 8


def mix_body(input_ref, cot_ref, weight_ref, *refs, planes, count):
    mixed_ref, skip_ref, total, spread = refs[-4:]
    step = pl.program_id(0)
    channels = input_ref.shape[0]
    side = channels * PLANES

    def pick(shape, axis):
        line = lax.broadcasted_iota(jnp.int32, shape, axis) // PLANES
        return line == lax.broadcasted_iota(jnp.int32, shape, 1 - axis)

    def same_plane():
        row = lax.broadcasted_iota(jnp.int32, (side, side), 0)
        column = lax.broadcasted_iota(jnp.int32, (side, side), 1)
        return row % PLANES == column % PLANES

    @pl.when(step == 0)
    def _():
        total[...] = jnp.zeros_like(total)
        tall = dot(pick((side, channels), 0).astype(BF16), weight_ref[...]).astype(BF16)
        wide = dot(tall, pick((channels, side), 1).astype(BF16))
        spread[...] = jnp.where(same_plane(), wide, 0.0).astype(BF16)

    mixed = [[] for _ in range(count)]
    for first in range(0, planes, PLANES):
        cots, lefts = [], []
        for k in range(count):
            rows = slice(k * planes, (k + 1) * planes)
            near = slice(first, first + PLANES)
            cots.append(cot_ref[:, rows, :].astype(F32)[:, near].reshape(side, NZ))
            lefts.append(input_ref[:, rows, :].astype(F32)[:, near].reshape(side, NZ))
        cot = jnp.concatenate(cots, axis=1).astype(BF16)
        left = jnp.concatenate(lefts, axis=1).astype(BF16)
        total[...] += lax.dot_general(
            left, cot, (((1,), (1,)), ((), ())), preferred_element_type=F32
        )
        found = dot(spread[...], cot)
        for k in range(count):
            mixed[k].append(found[:, k * NZ : (k + 1) * NZ].reshape(channels, PLANES, NZ))
    for k in range(count):
        mixed_ref[:, k * planes : (k + 1) * planes, :] = jnp.concatenate(
            mixed[k], axis=1
        ).astype(BF16)

    @pl.when(step == pl.num_programs(0) - 1)
    def _():
        kept = jnp.where(same_plane(), total[...], 0.0)
        half = lax.dot_general(
            kept,
            pick((side, LANES), 0).astype(F32),
            (((1,), (0,)), ((), ())),
            precision=lax.Precision.HIGHEST,
            preferred_element_type=F32,
        )
        skip_ref[...] = lax.dot_general(
            pick((channels, side), 1).astype(F32),
            half,
            (((1,), (0,)), ((), ())),
            precision=lax.Precision.HIGHEST,
            preferred_element_type=F32,
        )


def mix(inputs, cot, weight, planes, after=()):
    channels, rows, _ = inputs.shape
    count = 16
    side = channels * PLANES
    spec = pl.BlockSpec((channels, count * planes, NZ), lambda x: (0, x, 0))
    return pl.pallas_call(
        functools.partial(mix_body, planes=planes, count=count),
        out_shape=(
            jax.ShapeDtypeStruct(inputs.shape, BF16),
            jax.ShapeDtypeStruct((channels, LANES), F32),
        ),
        grid=(NX // count,),
        in_specs=[spec, spec, whole((channels, channels))] + [ANYWHERE] * len(after),
        out_specs=(spec, whole((channels, LANES))),
        scratch_shapes=[pltpu.VMEM((side, side), F32), pltpu.VMEM((side, side), BF16)],
        compiler_params=params(),
        cost_estimate=cost(22),
        name="mix",
    )(inputs, cot, weight, *after)


def x_then_z(
    received, mixed_ref, table_x, table_z, out_ref, real_ref, imag_ref, planes
):
    part = 2 * MX // len(received)
    for y in range(0, planes, 2):
        pair = [
            jnp.concatenate(
                [
                    ref[side, at * part : (at + 1) * part, :]
                    for side in range(2)
                    for ref in received
                ],
                axis=0,
            ).astype(BF16)
            for at in (y, y + 1)
        ]
        found = dot(table_x[0], jnp.concatenate(pair, axis=1))
        for place in range(2):
            lane = slice(place * LANES, (place + 1) * LANES)
            real_ref[pl.ds(y + place, NX, stride=planes), :] = found[:NX, lane]
            imag_ref[pl.ds(y + place, NX, stride=planes), :] = found[NX:, lane]
    rows = NX * planes
    step = min(rows, 256)
    for start in range(0, rows, step):
        place = slice(start, start + step)
        line = jnp.concatenate([real_ref[place, :], imag_ref[place, :]], axis=1).astype(BF16)
        found = dot(line, table_z[...])
        for c in range(GROUP):
            mixed = mixed_ref[c, place, :].astype(F32)
            out_ref[c, place, :] = (found[:, c * NZ : (c + 1) * NZ] + mixed).astype(BF16)


def grid_body(relay_ref, *refs, planes, relays, root):
    received, refs = refs[:relays], refs[relays:]
    if root is None:
        mixed_ref, table_x, table_z = refs[:3]
        out_ref, real_ref, imag_ref = refs[-3:]
    else:
        skips, refs = refs[:relays], refs[relays:]
        mixed_ref, table_x, table_z = refs[:3]
        out_ref, total_ref, real_ref, imag_ref = refs[-4:]

        @pl.when(pl.program_id(0) == 0)
        def _():
            total = sum(ref[0] for ref in skips)
            total_ref[...] = total[:, : total_ref.shape[1]] / root

    x_then_z(received, mixed_ref, table_x, table_z, out_ref, real_ref, imag_ref, planes)


def grid_of(relay, received, mixed, first, groups, planes, root=None, after=()):
    relays = len(received)
    channels = mixed.shape[0]
    per_group = planes * 2 * MX // relays
    spec = pl.BlockSpec((GROUP, NX * planes, NZ), lambda g, at: (g + first, 0, 0))
    in_specs = [pl.BlockSpec((2, per_group, LANES), lambda g, at: (0, g, 0))] * relays
    operands = list(received)
    out_shape = (jax.ShapeDtypeStruct(mixed.shape, BF16),)
    out_specs = (spec,)
    if root is not None:
        extra = groups * per_group // channels
        in_specs += [pl.BlockSpec((1, channels, LANES), lambda g, at: (0, extra, 0))] * relays
        operands += received
        out_shape += (jax.ShapeDtypeStruct((channels, channels), F32),)
        out_specs += (fixed((channels, channels)),)
    in_specs += [
        spec,
        pl.BlockSpec((1, 2 * NX, 4 * MX), lambda g, at: (at[0], 0, 0)),
        fixed((2 * LANES, GROUP * NZ)),
    ] + [ANYWHERE] * len(after)
    operands += [mixed, x_inverse_table(relays), z_inverse_table(), *after]
    return pl.pallas_call(
        functools.partial(grid_body, planes=planes, relays=relays, root=root),
        out_shape=out_shape,
        grid_spec=pltpu.PrefetchScalarGridSpec(
            num_scalar_prefetch=1,
            grid=(groups,),
            in_specs=in_specs,
            out_specs=out_specs,
            scratch_shapes=[
                pltpu.VMEM((NX * planes, LANES), F32),
                pltpu.VMEM((NX * planes, LANES), F32),
            ],
        ),
        input_output_aliases={1 + (relays if root is None else 2 * relays): 0},
        compiler_params=params(),
        cost_estimate=cost(9),
        name="to_grid",
    )(relay, *operands)


def cross_body(*refs, samples):
    lefts, rights, out_ref = refs[:samples], refs[samples : 2 * samples], refs[-1]
    channels, own, lanes = out_ref.shape[1:]
    kz = lax.broadcasted_iota(jnp.int32, (own, lanes), 1) // (2 * MY) % MZ
    scale = jnp.where(kz == 0, 1.0, 2.0) / float(NX * NY * NZ)
    scaled = [(ref[:own, :] * scale, ref[own : 2 * own, :] * scale) for ref in rights]
    for i in range(channels):
        real = imag = None
        for b in range(samples):
            left_real = lefts[b][i : i + 1, :]
            left_imag = lefts[b][channels + i : channels + i + 1, :]
            right_real, right_imag = scaled[b]
            one = left_real * right_real + left_imag * right_imag
            two = left_real * right_imag - left_imag * right_real
            real = one if real is None else real + one
            imag = two if imag is None else imag + two
        out_ref[0, i] = real
        out_ref[1, i] = imag


def cross(lefts, rights, after=()):
    rows, modes = lefts[0].shape
    channels = rows // 2
    own = (rights[0].shape[0] - SUBLANES) // 2
    lanes = 2 * MY * MZ
    return pl.pallas_call(
        functools.partial(cross_body, samples=len(lefts)),
        out_shape=jax.ShapeDtypeStruct((2, channels, own, modes), F32),
        grid=(modes // lanes,),
        in_specs=[pl.BlockSpec((rows, lanes), lambda k: (0, k))] * len(lefts)
        + [pl.BlockSpec((2 * own + SUBLANES, lanes), lambda k: (0, k))] * len(rights)
        + [ANYWHERE] * len(after),
        out_specs=pl.BlockSpec((2, channels, own, lanes), lambda k: (0, 0, 0, k)),
        compiler_params=params(),
        cost_estimate=cost(6),
        name="cross",
    )(*lefts, *rights, *after)


def exchange_near(values):
    spaces = lax.axis_size("space")
    groups = [list(range(spaces // 2)), list(range(spaces // 2, spaces))]
    return lax.all_to_all(
        values, "space", split_axis=0, concat_axis=0, axis_index_groups=groups, tiled=True
    )


def spread(blocks, axis):
    size = lax.axis_size(axis)
    return [blocks[0]] + [
        lax.ppermute(blocks[d], axis, [(s, s ^ d) for s in range(size)])
        for d in range(1, len(blocks))
    ]


def exchange_far(values, turned=False):
    spaces = lax.axis_size("space")
    pairs = [(s, (s + spaces // 2) % spaces) for s in range(spaces)]
    pairs = pairs[::-1] if turned else pairs
    return lax.ppermute(values, "space", pairs)


HIGHEST = lax.Precision.HIGHEST


def phase_table(length, count, signed):
    points = jnp.arange(length, dtype=jnp.int32)
    orders = jnp.arange(count, dtype=jnp.int32)
    if signed:
        orders = jnp.where(orders < count // 2, orders, orders - count)
    residues = jnp.mod(points[:, None] * orders[None, :], length)
    radians = residues.astype(jnp.float32) * (2.0 * math.pi / length)
    return (jnp.cos(radians), jnp.sin(radians))


def forward_block(cosine, sine):
    return jnp.stack(
        [jnp.stack([cosine, -sine], axis=1), jnp.stack([sine, cosine], axis=1)], axis=0
    )


def inverse_block(cosine, sine):
    cos_rows = cosine.T
    sin_rows = sine.T
    return jnp.stack(
        [jnp.stack([cos_rows, sin_rows], axis=1), jnp.stack([-sin_rows, cos_rows], axis=1)], axis=0
    )


def local_spectrum(grid_in):
    cos_x, sin_x = phase_table(NX, 2 * MX, True)
    table_x = jnp.stack([cos_x, -sin_x], axis=1).astype(jnp.bfloat16)
    section_x = jnp.einsum(
        "scxyz,xpa->scpayz", grid_in, table_x, preferred_element_type=jnp.float32
    )
    cos_z, sin_z = phase_table(NZ, MZ, False)
    section_z = jnp.einsum(
        "scpayz,pzqk->scqyak", section_x, forward_block(cos_z, sin_z), precision=HIGHEST
    )
    return section_z.reshape(
        section_z.shape[0], section_z.shape[1], 2, section_z.shape[3], 2 * MX * MZ
    )


def along_y(spectra):
    cos_y, sin_y = phase_table(NY, 2 * MY, True)
    section_y = jnp.einsum(
        "scpym,pyqk->scqmk", spectra, forward_block(cos_y, sin_y), precision=HIGHEST
    )
    return section_y.reshape(section_y.shape[0], section_y.shape[1], 2, section_y.shape[3] * 2 * MY)


def both_along_y(spectra_pair):
    return (along_y(spectra_pair[0]), along_y(spectra_pair[1]))


def to_grid(spectra):
    shaped = spectra.reshape(spectra.shape[0], spectra.shape[1], 2, spectra.shape[3], 2 * MX, MZ)
    cos_z, sin_z = phase_table(NZ, MZ, False)
    grid_z = jnp.einsum(
        "scpyak,pkqz->scqayz", shaped, inverse_block(cos_z, sin_z), precision=HIGHEST
    )
    cos_x, sin_x = phase_table(NX, 2 * MX, True)
    table_x = jnp.stack([cos_x.T, -sin_x.T], axis=0)
    return jnp.einsum("scpayz,pax->scxyz", grid_z, table_x, precision=HIGHEST)


def cross_terms(spec_left, spec_right):
    real_part = jnp.einsum(
        "sim,som->iom", spec_left[:, :, 0], spec_right[:, :, 0], precision=HIGHEST
    )
    real_part = real_part + jnp.einsum(
        "sim,som->iom", spec_left[:, :, 1], spec_right[:, :, 1], precision=HIGHEST
    )
    imag_part = jnp.einsum(
        "sim,som->iom", spec_left[:, :, 0], spec_right[:, :, 1], precision=HIGHEST
    )
    imag_part = imag_part - jnp.einsum(
        "sim,som->iom", spec_left[:, :, 1], spec_right[:, :, 0], precision=HIGHEST
    )
    return jnp.stack([real_part, imag_part], axis=0)


def contract(weight_part, spec_part):
    return jnp.einsum("iom,som->sim", weight_part, spec_part, preferred_element_type=jnp.float32)


def skip_gradient(grid_in, cot_pre):
    partial_sum = jnp.einsum(
        "sixyz,soxyz->io", grid_in, cot_pre, preferred_element_type=jnp.float32
    )
    summed = lax.psum(partial_sum, ("batch", "space"))
    return summed / math.sqrt(grid_in.shape[0] * lax.axis_size("batch") * NX * NY * NZ)


def general(inputs, pre_act, cotangent, spectral_weight, skip_weight):
    samples = inputs.shape[0]
    channels = inputs.shape[1]
    slope_pre = slope(pre_act.astype(jnp.float32))
    cot_pre = (cotangent.astype(jnp.float32) * slope_pre).astype(jnp.bfloat16)
    spec_u, spec_e = both_along_y(
        (
            lax.all_to_all(
                local_spectrum(inputs), "space", split_axis=4, concat_axis=3, tiled=True
            ),
            lax.all_to_all(
                local_spectrum(cot_pre), "space", split_axis=4, concat_axis=3, tiled=True
            ),
        )
    )
    mode_count = spec_u.shape[3]
    position = jnp.arange(mode_count, dtype=jnp.int32)
    kxz_index = lax.axis_index("space") * (mode_count // (2 * MY)) + position // (2 * MY)
    mode_weights = jnp.where(kxz_index % MZ == 0, 1.0, 2.0).astype(jnp.float32) / float(
        NX * NY * NZ
    )
    mode_grad = lax.psum_scatter(
        cross_terms(spec_u, spec_e), "batch", scatter_dimension=2, tiled=True
    )
    grad_spectral = mode_grad * mode_weights
    rounded = spec_e.astype(jnp.bfloat16)
    weight_real = spectral_weight[0]
    weight_imag = spectral_weight[1]
    back_real = contract(weight_real, rounded[:, :, 0]) + contract(weight_imag, rounded[:, :, 1])
    back_imag = contract(weight_real, rounded[:, :, 1]) - contract(weight_imag, rounded[:, :, 0])
    back_modes = jnp.stack([back_real, back_imag], axis=2) * mode_weights
    shaped = back_modes.reshape(samples, channels, 2, mode_count // (2 * MY), 2 * MY)
    cos_y, sin_y = phase_table(NY, 2 * MY, True)
    grid_y = jnp.einsum("scpmk,pkqy->scqym", shaped, inverse_block(cos_y, sin_y), precision=HIGHEST)
    spatial = to_grid(lax.all_to_all(grid_y, "space", split_axis=3, concat_axis=4, tiled=True))
    mixed = jnp.einsum("io,soxyz->sixyz", skip_weight, cot_pre, preferred_element_type=jnp.float32)
    grad_inputs = (spatial + mixed).astype(jnp.bfloat16)
    grad_skip = skip_gradient(inputs, cot_pre)
    return (grad_inputs, grad_spectral, grad_skip)


def on_device(inputs, pre_act, cotangent, spectral_weight, skip_weight):
    samples, channels, _, planes, _ = inputs.shape
    spaces = lax.axis_size("space")
    batches = lax.axis_size("batch")
    if samples != 1 or spaces < 2 or spaces & (spaces - 1) or (2 * MX) % spaces or planes % 16 or channels % (4 * GROUP):
        return general(inputs, pre_act, cotangent, spectral_weight, skip_weight)
    if batches & (batches - 1) or channels % (SUBLANES * batches):
        return general(inputs, pre_act, cotangent, spectral_weight, skip_weight)
    kx_local = 2 * MX // spaces
    flat = (channels, NX * planes, NZ)
    groups = channels // GROUP
    inputs, pre_act, cotangent = (v.reshape(flat) for v in (inputs, pre_act, cotangent))
    half = (lax.axis_index("space") // (spaces // 2)).astype(jnp.int32).reshape(1)
    relay = (lax.axis_index("space") % (spaces // 2)).astype(jnp.int32).reshape(1)
    batch = lax.axis_index("batch").astype(jnp.int32).reshape(1)
    middle = groups // 2
    (send_u,) = forward((inputs,), 0, groups, planes, spaces, False)
    near_u = exchange_near(send_u)
    send_e, cot_pre = forward(
        (pre_act, cotangent), 0, groups, planes, spaces, True, after=(send_u,)
    )
    near_e = exchange_near(send_e)
    part_u = partial_sums(half, near_u, groups, kx_local, "partial_u", after=(send_e,))
    far_u = exchange_far(part_u)
    mixed, skip_part = mix(inputs, cot_pre, skip_weight, planes, after=(part_u,))
    part_e = partial_sums(half, near_e, groups, kx_local, "partial_e", riding=(skip_part,))
    far_e = exchange_far(part_e)
    hat_u = finish_u(half, near_u, far_u, channels, kx_local, after=(part_e,))
    all_u = spread([hat_u] * batches, "batch")
    own_e, rounded, modes_a = finish_e(
        batch, half, near_e, far_e, spectral_weight, skip_part, kx_local, batches, (hat_u,)
    )
    far_a = exchange_far(modes_a)
    all_e = spread(own_e, "batch")
    modes_b = finish_rest(rounded, spectral_weight, kx_local, after=tuple(all_u[1:]))
    modes_b, far_a = lax.optimization_barrier((modes_b, far_a))
    far_b = exchange_far(modes_b, turned=True)
    send_a = expand(half, relay, modes_a, far_a, spaces // 2, middle, kx_local)
    near_a = spread(send_a, "space")
    grad_spectral = cross(all_u, all_e, after=send_a[:1])
    send_b = expand(
        half,
        relay,
        modes_b,
        far_b,
        spaces // 2,
        middle,
        kx_local,
        all_e,
        channels,
        (grad_spectral,),
    )
    near_b = spread(send_b, "space")
    (grad_inputs,) = grid_of(relay, near_a, mixed, 0, middle, planes, after=send_b[:1])
    root = math.sqrt(samples * batches * NX * NY * NZ)
    grad_inputs, grad_skip = grid_of(relay, near_b, grad_inputs, middle, middle, planes, root)
    return (
        grad_inputs.reshape(samples, channels, NX, planes, NZ),
        grad_spectral,
        grad_skip,
    )


def solution(mesh):
    placed = (
        P("batch", None, None, "space", None),
        P("batch", None, None, "space", None),
        P("batch", None, None, "space", None),
        P(None, None, None, "space"),
        P(),
    )
    return jax.shard_map(
        on_device,
        mesh=mesh,
        in_specs=placed,
        out_specs=(P("batch", None, None, "space", None), P(None, None, "batch", "space"), P()),
        check_vma=False,
    )
```
